32 devices in a mesh: dp: 8 (over y, x, core), tensor: 4 (over z).
Axes of the slice: x: 2, y: 2, z: 4, core: 2. Of those that a mesh axis runs over, the one named last changes fastest.
Arguments:
- latents: bfloat16 [16, 256, 768], P('dp'), may hold values from -6 to 6
- condition: bfloat16 [16, 768], P('dp', 'tensor'), may hold values from -6 to 6
- modulator: bfloat16 [768, 4608], P('tensor'), may hold values from -0.21875 to 0.21875
- modulator_bias: bfloat16 [4608], replicated, may hold values from -1.5 to 1.5
- attn_input: bfloat16 [3, 768, 768], P(None, None, 'tensor'), may hold values from -0.21875 to 0.21875
- attn_input_bias: bfloat16 [2, 768], P(None, 'tensor'), may hold values from -2.5 to 2.5
- attn_output: bfloat16 [768, 768], P('tensor'), may hold values from -1.75 to 1.75
- attn_output_bias: bfloat16 [768], replicated, may hold values from -2.5 to 2.5
- ffn_input: bfloat16 [768, 3072], P(None, 'tensor'), may hold values from -0.21875 to 0.21875
- ffn_input_bias: bfloat16 [3072], P('tensor'), may hold values from -2.5 to 2.5
- ffn_output: bfloat16 [3072, 768], P('tensor'), may hold values from -0.109375 to 0.109375
- ffn_output_bias: bfloat16 [768], replicated, may hold values from -2.5 to 2.5
- cotangent: bfloat16 [16, 256, 768], P('dp'), may hold values from -6 to 6
Outputs:
- layer_out: bfloat16 [16, 256, 768], P('dp')
- latents_grad: float32 [16, 256, 768], P('dp')
- condition_grad: float32 [16, 768], P('dp', 'tensor')
- modulator_grad: float32 [768, 4608], P('tensor')
- modulator_bias_grad: float32 [4608], replicated
- attn_input_grad: float32 [3, 768, 768], P(None, None, 'tensor')
- attn_input_bias_grad: float32 [2, 768], P(None, 'tensor')
- attn_output_grad: float32 [768, 768], P('tensor')
- attn_output_bias_grad: float32 [768], replicated
- ffn_input_grad: float32 [768, 3072], P(None, 'tensor')
- ffn_input_bias_grad: float32 [3072], P('tensor')
- ffn_output_grad: float32 [3072, 768], P('tensor')
- ffn_output_bias_grad: float32 [768], replicated
The draws below stay inside these ranges and needn't reach their ends.
All inputs are finite; a program needn't handle non-finite values.
Results may differ from the reference program's by a relative error of at most 0.014.
The reference program's roundings to bfloat16 on the way count: a program that leaves them out, or rounds other values in their place, can miss the bound.
Values sent between devices are 32-bit elements; how exact they have to be, the bound alone decides.
No kernel may reach another device: no remote copies, remote signals or barrier semaphores. Data moves between devices by JAX's collectives and lax.ppermute only.
A program may use at most 128 MiB of HBM per device.

```python
import jax
import jax.numpy as jnp
from jax import lax

D = 768
HEADS = 12
HEAD = 64
FF = 3072
SEQ = 256
IMG_DEV = 2
IMAGES = 16
N_DP = 8


def block_levels(key, dims, shards, low, largest):
    loudness = 1.0
    for position, shards_of in shards:
        draws = jax.random.uniform(jax.random.fold_in(jax.random.fold_in(key, 6), position), (shards_of,), jnp.float32, low / len(shards), largest / len(shards))
        loudness = loudness * jnp.repeat(jnp.exp(draws), dims[position] // shards_of).reshape((-1,) + (1,) * (len(dims) - 1 - position))
    return loudness


def gaussian(stream_key, dims, scale, bound, cuts=(), dtype=jnp.bfloat16):
    drawn = jax.random.normal(stream_key, dims, jnp.float32) * scale
    if len(cuts) > 0:
        drawn = block_levels(stream_key, dims, cuts, -0.22, 0.18) * drawn
    return jnp.clip(drawn, min=-bound, max=bound).astype(dtype)


def setup_inputs(seed: int = 0) -> dict:
    key_list = jax.random.split(jax.random.key(seed), 14)
    return {
        "latents": gaussian(key_list[0], (IMAGES, SEQ, D), 1.0, 6.0, ((0, 8),)),
        "condition": gaussian(key_list[1], (IMAGES, D), 1.0, 6.0, ((0, 8), (1, 4))),
        "modulator": gaussian(key_list[2], (D, 6 * D), D ** -0.5, 0.21875, ((0, 4),)),
        "modulator_bias": gaussian(key_list[3], (6 * D,), 0.3, 1.5),
        "attn_input": gaussian(key_list[4], (3, D, D), D ** -0.5, 0.21875, ((2, 4),)),
        "attn_input_bias": gaussian(key_list[5], (2, D), 0.5, 2.5, ((1, 4),)),
        "attn_output": gaussian(key_list[6], (D, D), (4 * D // SEQ) ** -0.5, 1.75, ((0, 4),)),
        "attn_output_bias": gaussian(key_list[7], (D,), 0.5, 2.5),
        "ffn_input": gaussian(key_list[8], (D, FF), D ** -0.5, 0.21875, ((1, 4),)),
        "ffn_input_bias": gaussian(key_list[9], (FF,), 0.5, 2.5, ((0, 4),)),
        "ffn_output": gaussian(key_list[10], (FF, D), FF ** -0.5, 0.109375, ((0, 4),)),
        "ffn_output_bias": gaussian(key_list[11], (D,), 0.5, 2.5),
        "cotangent": gaussian(key_list[12], (IMAGES, SEQ, D), 1.0, 6.0, ((0, 8),)),
    }


@jax.custom_vjp
def low(v):
    return lax.optimization_barrier(v.astype(jnp.bfloat16)).astype(jnp.float32)

@jax.custom_vjp
def low_back(v):
    return v

def low_keep(v):
    return (low(v), None)

def low_pass(kept, grad):
    return (grad,)

def back_keep(v):
    return (v, None)

def back_low(kept, grad):
    return (low(grad),)
low.defvjp(low_keep, low_pass)
low_back.defvjp(back_keep, back_low)
epsilon = 1e-06

def matmul(left, right):
    return jnp.dot(left, right, precision=lax.Precision.HIGHEST, preferred_element_type=jnp.float32)

def contract(form, left, right):
    return jnp.einsum(form, left, right, precision=lax.Precision.HIGHEST)

def layer_norm(values):
    centre = values - lax.optimization_barrier(jnp.mean(values, axis=-1, keepdims=True))
    spread = lax.optimization_barrier(jnp.mean(centre * centre, axis=-1, keepdims=True))
    return centre * lax.rsqrt(spread + epsilon)

def forward(latents, condition, modulator, modulator_bias, attn_input, attn_input_bias, attn_output, attn_output_bias, ffn_input, ffn_input_bias, ffn_output, ffn_output_bias):
    groups = latents.shape[0]
    context = low(jax.nn.silu(condition))
    modulation = low_back(matmul(context, modulator) + modulator_bias)
    pieces = modulation.reshape(groups, 6, D)[:, None]
    shift_one, scale_one, gate_one = (pieces[:, :, 0], pieces[:, :, 1], pieces[:, :, 2])
    shift_two, scale_two, gate_two = (pieces[:, :, 3], pieces[:, :, 4], pieces[:, :, 5])
    entry_one = low(layer_norm(latents) * (1.0 + scale_one) + shift_one).reshape(-1, D)

    def project(weight, offset):
        return low_back(low(matmul(entry_one, weight) + offset)).reshape(groups, SEQ, HEADS, HEAD)
    query = project(attn_input[0], attn_input_bias[0])
    keys = project(attn_input[1], jnp.zeros((D,), jnp.float32))
    values = project(attn_input[2], attn_input_bias[1])
    scores = low_back(contract('gqhe,gkhe->ghqk', query, keys) * HEAD ** (-0.5))
    probs = low(jax.nn.softmax(scores, axis=-1))
    mixed = low_back(low(contract('ghqk,gkhe->gqhe', probs, values)))
    attention = low_back(matmul(mixed.reshape(-1, D), attn_output) + attn_output_bias).reshape(groups, SEQ, D)
    middle = latents + gate_one * attention
    entry_two = low(layer_norm(middle) * (1.0 + scale_two) + shift_two).reshape(-1, D)
    hidden = low_back(matmul(entry_two, ffn_input) + ffn_input_bias)
    active = low(jax.nn.gelu(hidden, approximate=True))
    branch = low_back(matmul(active, ffn_output) + ffn_output_bias).reshape(groups, SEQ, D)
    return middle + gate_two * branch

def reference(latents, condition, modulator, modulator_bias, attn_input, attn_input_bias, attn_output, attn_output_bias, ffn_input, ffn_input_bias, ffn_output, ffn_output_bias, cotangent):
    weights = tuple((w.astype(jnp.float32) for w in (modulator, modulator_bias, attn_input, attn_input_bias, attn_output, attn_output_bias, ffn_input, ffn_input_bias, ffn_output, ffn_output_bias)))
    image_groups = latents.astype(jnp.float32).reshape(N_DP, IMG_DEV, SEQ, D)
    cond_groups = condition.astype(jnp.float32).reshape(N_DP, IMG_DEV, D)
    cot_groups = cotangent.astype(jnp.float32).reshape(N_DP, IMG_DEV, SEQ, D)

    def one_group(totals, inputs):
        image_part, cond_part, cot_part = inputs
        result, pullback = jax.vjp(forward, image_part, cond_part, *weights)
        grads = pullback(cot_part)
        totals = tuple((total + grad for total, grad in zip(totals, grads[2:])))
        return (totals, (result.astype(jnp.bfloat16), grads[0], grads[1]))
    zeros = tuple((jnp.zeros(weight.shape, jnp.float32) for weight in weights))
    totals, (results, image_grads, cond_grads) = lax.scan(one_group, zeros, (image_groups, cond_groups, cot_groups))
    return (results.reshape(IMAGES, SEQ, D), image_grads.reshape(IMAGES, SEQ, D), cond_grads.reshape(IMAGES, D), totals[0], totals[1], totals[2], totals[3], totals[4], totals[5], totals[6], totals[7], totals[8], totals[9])
```

```python
import functools

import jax
import jax.numpy as jnp
from jax import lax
from jax.experimental import pallas as pl
from jax.experimental.pallas import tpu as pltpu
from jax.sharding import PartitionSpec as P

HEAD = 64
epsilon = 1e-06
SCALE = HEAD ** (-0.5)
LOW = jnp.bfloat16
FULL = jnp.float32
NN = (((1,), (0,)), ((), ()))
NT = (((1,), (1,)), ((), ()))
TN = (((0,), (0,)), ((), ()))


def mm(left, right, dims=NN):
    return lax.dot_general(left, right, dims, preferred_element_type=FULL)


def norm_parts(values):
    centre = values - jnp.mean(values, axis=-1, keepdims=True)
    inverse = lax.rsqrt(jnp.mean(centre * centre, axis=-1, keepdims=True) + epsilon)
    return (centre * inverse, inverse)


def norm_back(grad, normed, inverse):
    return (
        grad
        - jnp.mean(grad, axis=-1, keepdims=True)
        - normed * jnp.mean(grad * normed, axis=-1, keepdims=True)
    ) * inverse


def softmax_t(keys_t, query_t):
    scores = mm(keys_t, query_t, TN) * SCALE
    shifted = jnp.exp(scores - jnp.max(scores, axis=0, keepdims=True))
    return shifted * (1.0 / jnp.sum(shifted, axis=0, keepdims=True))


def forward_kernel(images, entry_ref, weight_ref, bias_ref, out_ref):
    columns = weight_ref.shape[1]
    positions = entry_ref.shape[0] // images
    entry = entry_ref[...]
    query, keys, values = (
        (mm(weight_ref[j], entry, NT) + bias_ref[j]).astype(LOW) for j in range(3)
    )
    for g in range(images):
        token = slice(g * positions, (g + 1) * positions)
        for h in range(columns // HEAD):
            row = slice(h * HEAD, (h + 1) * HEAD)
            probs = softmax_t(keys[row, token], query[row, token])
            mixed = mm(values[row, token], probs.astype(LOW))
            out_ref[row, token] = mixed.astype(LOW).astype(FULL)


def attention_forward(entry, weight_t, bias, images):
    tokens = entry.shape[0]
    columns = weight_t.shape[1]
    return pl.pallas_call(
        functools.partial(forward_kernel, images),
        out_shape=jax.ShapeDtypeStruct((columns, tokens), FULL),
        compiler_params=pltpu.CompilerParams(vmem_limit_bytes=48 * 2**20),
        name="attention_forward",
    )(entry, weight_t, bias)


def backward_kernel(heads, proj_ref, grad_ref, out_ref):
    for h in range(heads):
        row = slice(h * HEAD, (h + 1) * HEAD)
        query, keys, values = proj_ref[0, row, :], proj_ref[1, row, :], proj_ref[2, row, :]
        grad = grad_ref[row, :]
        probs = softmax_t(keys, query)
        probs_grad = mm(values, grad, TN)
        weighted = probs * probs_grad
        scores_grad = (weighted - probs * jnp.sum(weighted, axis=0, keepdims=True)).astype(LOW)
        out_ref[0, row, :] = (mm(keys, scores_grad) * SCALE).astype(LOW)
        out_ref[1, row, :] = (mm(query, scores_grad, NT) * SCALE).astype(LOW)
        out_ref[2, row, :] = mm(grad, probs.astype(LOW), NT).astype(LOW)


def attention_backward(proj_t, grad_t, images):
    width, tokens = grad_t.shape
    positions = tokens // images
    heads = width // HEAD
    step = 4 if heads % 4 == 0 else heads
    rows = step * HEAD
    return pl.pallas_call(
        functools.partial(backward_kernel, step),
        out_shape=jax.ShapeDtypeStruct((3, width, tokens), LOW),
        grid=(images, heads // step),
        in_specs=[
            pl.BlockSpec((3, rows, positions), lambda g, h: (0, h, g)),
            pl.BlockSpec((rows, positions), lambda g, h: (h, g)),
        ],
        out_specs=pl.BlockSpec((3, rows, positions), lambda g, h: (0, h, g)),
        compiler_params=pltpu.CompilerParams(vmem_limit_bytes=48 * 2**20),
        name="attention_backward",
    )(proj_t, grad_t)


def join_kernel(mixed_ref, weight_ref, bias_ref, inputs_ref, mod_ref, attention_ref, middle_ref, entry_ref, low_ref):
    weight = weight_ref[...].astype(LOW)
    low_ref[...] = weight
    attention = mm(mixed_ref[...].astype(LOW), weight, TN) + bias_ref[...].astype(FULL)
    attention_ref[...] = attention
    middle = inputs_ref[...].astype(FULL) + mod_ref[0, 2:3, :] * attention
    middle_ref[...] = middle
    normed = norm_parts(middle)[0]
    entry_ref[...] = (normed * (1.0 + mod_ref[0, 4:5, :]) + mod_ref[0, 3:4, :]).astype(LOW)


def join_heads(mixed, weight, bias, inputs, modulation):
    images = modulation.shape[0]
    tokens, width = inputs.shape
    positions = tokens // images
    by_image = pl.BlockSpec((positions, width), lambda g: (g, 0))
    whole = pl.BlockSpec(weight.shape, lambda g: (0, 0))
    return pl.pallas_call(
        join_kernel,
        out_shape=(
            jax.ShapeDtypeStruct((tokens, width), FULL),
            jax.ShapeDtypeStruct((tokens, width), FULL),
            jax.ShapeDtypeStruct((tokens, width), LOW),
            jax.ShapeDtypeStruct(weight.shape, LOW),
        ),
        grid=(images,),
        in_specs=[
            pl.BlockSpec((weight.shape[0], positions), lambda g: (0, g)),
            whole,
            pl.BlockSpec((1, width), lambda g: (0, 0)),
            by_image,
            pl.BlockSpec((1, 6, width), lambda g: (g, 0, 0)),
        ],
        out_specs=(by_image, by_image, by_image, whole),
        compiler_params=pltpu.CompilerParams(vmem_limit_bytes=48 * 2**20),
        name="join_heads",
    )(mixed, weight, bias, inputs, modulation)


def project_kernel(weight_ref, bias_ref, entry_ref, out_ref, low_ref):
    weight = weight_ref[0, 0].astype(LOW)
    low_ref[0] = weight
    out_ref[0] = (mm(weight, entry_ref[...], NT) + bias_ref[0]).astype(LOW)


def project_all(weight, bias, entry):
    groups, _, columns, width = weight.shape
    tokens = entry.shape[0]
    return pl.pallas_call(
        project_kernel,
        out_shape=(
            jax.ShapeDtypeStruct((3, groups * columns, tokens), LOW),
            jax.ShapeDtypeStruct((3, groups * columns, width), LOW),
        ),
        grid=(3, groups),
        in_specs=[
            pl.BlockSpec((1, 1, columns, width), lambda j, t: (t, j, 0, 0)),
            pl.BlockSpec((1, columns, 1), lambda j, t: (j, t, 0)),
            pl.BlockSpec((tokens, width), lambda j, t: (0, 0)),
        ],
        out_specs=(
            pl.BlockSpec((1, columns, tokens), lambda j, t: (j, t, 0)),
            pl.BlockSpec((1, columns, width), lambda j, t: (j, t, 0)),
        ),
        compiler_params=pltpu.CompilerParams(vmem_limit_bytes=48 * 2**20),
        name="project_all",
    )(weight, bias, entry)


def flip(value, axis, count, mask):
    return lax.ppermute(value, axis, [(i, i ^ mask) for i in range(count)])


def flip_sum(value, axis, count):
    parts = [value] + [flip(value, axis, count, mask) for mask in range(1, count)]
    while len(parts) > 1:
        parts = [a + b for a, b in zip(parts[::2], parts[1::2])]
    return parts[0]


def halving_sum(value, axis, count, masks):
    place = lax.axis_index(axis)
    for mask in masks:
        half = value.shape[0] // 2
        side = (place // mask) % 2
        away = lax.dynamic_slice_in_dim(value, (1 - side) * half, half, 0)
        kept = lax.dynamic_slice_in_dim(value, side * half, half, 0)
        value = kept + flip(away, axis, count, mask)
    for mask in reversed(masks):
        other = flip(value, axis, count, mask)
        lower = (place // mask) % 2 == 0
        value = jnp.concatenate([jnp.where(lower, value, other), jnp.where(lower, other, value)])
    return value


def pair_sum(one, two, axis, count):
    masks = [1 << i for i in range(count.bit_length() - 1)]
    one = halving_sum(one, axis, count, masks)
    return one, halving_sum(two, axis, count, masks[:1] + masks[:0:-1])


def gather_rows(rows, n_dp):
    share = rows.shape[0] // n_dp
    mine = lax.dynamic_slice_in_dim(rows, lax.axis_index("dp") * share, share, 0)
    return lax.all_gather(mine.astype(FULL), ("tensor", "dp"), tiled=True)


def per_device(
    n_dp,
    n_tensor,
    latents,
    condition,
    modulator,
    modulator_bias,
    attn_input,
    attn_input_bias,
    attn_output,
    attn_output_bias,
    ffn_input,
    ffn_input_bias,
    ffn_output,
    ffn_output_bias,
    cotangent,
):
    image_count, positions, features = latents.shape
    tokens = image_count * positions
    columns = attn_input.shape[2]
    place = lax.axis_index("tensor")

    weight_t = attn_input.swapaxes(1, 2)
    output_wide = gather_rows(attn_output, n_dp)
    weight_wide = gather_rows(weight_t.reshape(-1, features), n_dp)
    weight_wide = weight_wide.reshape(n_tensor, 3, columns, features)
    in_bias = attn_input_bias.astype(FULL)
    bias_own = jnp.stack([in_bias[0], jnp.zeros_like(in_bias[0]), in_bias[1]])
    bias_full = lax.all_gather(bias_own, "tensor", axis=1, tiled=True)

    cond_float = condition.astype(FULL)
    context_low = jax.nn.silu(cond_float).astype(LOW)
    modulation = flip_sum(mm(context_low, modulator), "tensor", n_tensor)
    modulation = modulation + modulator_bias.astype(FULL)
    pieces = modulation.reshape(image_count, 6, features)[:, None]
    shift_one, scale_one, gate_one = (pieces[:, :, 0], pieces[:, :, 1], pieces[:, :, 2])
    shift_two, scale_two, gate_two = (pieces[:, :, 3], pieces[:, :, 4], pieces[:, :, 5])
    inputs = latents.astype(FULL)
    normed_one, inverse_one = norm_parts(inputs)
    entry_one = (normed_one * (1.0 + scale_one) + shift_one).astype(LOW).reshape(-1, features)
    mixed_t = attention_forward(entry_one, weight_t, bias_own[:, :, None], image_count)
    mixed_full = lax.all_gather(mixed_t, "tensor", tiled=True)
    attention, middle, entry_two, output_full = join_heads(
        mixed_full,
        output_wide,
        attn_output_bias[None],
        latents.reshape(-1, features),
        modulation.reshape(image_count, 6, features),
    )
    attention = attention.reshape(latents.shape)
    middle = middle.reshape(latents.shape)
    normed_two, inverse_two = norm_parts(middle)
    hidden = mm(entry_two, ffn_input) + ffn_input_bias.astype(FULL)
    active, gelu_pull = jax.vjp(lambda inner: jax.nn.gelu(inner, approximate=True), hidden)
    active = active.astype(LOW)
    upstream = cotangent.astype(FULL)
    branch_grad = (gate_two * upstream).astype(LOW).reshape(-1, features)
    active_grad = mm(branch_grad, ffn_output, NT)
    hidden_grad = gelu_pull(active_grad)[0].astype(LOW)
    entry_two_grad = lax.psum(mm(hidden_grad, ffn_input, NT), "tensor").reshape(latents.shape)
    branch = lax.psum_scatter(mm(active, ffn_output), "tensor", tiled=True)
    branch = lax.all_gather(branch, "tensor", tiled=True)
    grad_ffn_output, grad_ffn_input = pair_sum(
        mm(active, branch_grad, TN), mm(entry_two, hidden_grad, TN), "dp", n_dp
    )
    grad_ffn_output_bias = jnp.sum(branch_grad.astype(FULL), axis=0)
    grad_ffn_input_bias = jnp.sum(hidden_grad.astype(FULL), axis=0)

    proj_full, weight_full = project_all(weight_wide, bias_full[:, :, None], entry_one)

    branch = (branch + ffn_output_bias.astype(FULL)).reshape(latents.shape)
    layer_out = (middle + gate_two * branch).astype(LOW)
    gate_two_grad = jnp.sum(upstream * branch, axis=1)

    scale_two_grad = jnp.sum(entry_two_grad * normed_two, axis=1)
    shift_two_grad = jnp.sum(entry_two_grad, axis=1)
    middle_grad = upstream + norm_back(entry_two_grad * (1.0 + scale_two), normed_two, inverse_two)
    gate_one_grad = jnp.sum(middle_grad * attention, axis=1)
    attention_grad = (gate_one * middle_grad).astype(LOW).reshape(-1, features)
    grad_attn_output = mm(mixed_t.astype(LOW), attention_grad)
    grad_attn_output_bias = jnp.sum(attention_grad.astype(FULL), axis=0)
    mixed_grad_t = mm(output_full, attention_grad, NT).astype(LOW)
    proj_grad = attention_backward(proj_full, mixed_grad_t, image_count)
    own = lax.dynamic_slice_in_dim(proj_grad, place * columns, columns, 1)
    grad_attn_input = mm(own.reshape(-1, tokens), entry_one)
    own_sums = jnp.sum(own.astype(FULL), axis=2)
    grad_attn_input_bias = jnp.stack([own_sums[0], own_sums[2]])
    attn_grads = jnp.concatenate([grad_attn_input, grad_attn_output])
    half = attn_grads.shape[0] // 2
    attn_grads = jnp.concatenate(pair_sum(attn_grads[:half], attn_grads[half:], "dp", n_dp))
    grad_attn_input = attn_grads[: 3 * columns].reshape(3, columns, features).swapaxes(1, 2)
    grad_attn_output = attn_grads[3 * columns :]

    entry_one_grad = mm(
        proj_grad.reshape(-1, tokens), weight_full.reshape(-1, features), TN
    ).reshape(latents.shape)
    scale_one_grad = jnp.sum(entry_one_grad * normed_one, axis=1)
    shift_one_grad = jnp.sum(entry_one_grad, axis=1)
    latents_grad = middle_grad + norm_back(
        entry_one_grad * (1.0 + scale_one), normed_one, inverse_one
    )
    modulation_grad = jnp.concatenate(
        [
            shift_one_grad,
            scale_one_grad,
            gate_one_grad,
            shift_two_grad,
            scale_two_grad,
            gate_two_grad,
        ],
        axis=-1,
    ).astype(LOW)
    context_grad = mm(modulation_grad, modulator, NT)
    condition_grad = jax.vjp(jax.nn.silu, cond_float)[1](context_grad)[0]

    small = jnp.concatenate(
        [
            modulation_grad.astype(FULL).reshape(-1),
            context_low.astype(FULL).reshape(-1),
            grad_ffn_output_bias,
            grad_ffn_input_bias,
            grad_attn_output_bias,
            grad_attn_input_bias.reshape(-1),
        ]
    )
    sizes = [image_count * 6 * features, image_count * condition.shape[1]]
    sizes += [features, ffn_input.shape[1], features, 2 * columns]
    spread = lax.optimization_barrier(lax.all_gather(small, "dp"))
    cuts = [sum(sizes[: i + 1]) for i in range(len(sizes) - 1)]
    every = jnp.split(spread, cuts, axis=1)
    all_modulation = every[0].reshape(-1, 6 * features)
    all_context = every[1].reshape(-1, condition.shape[1])
    grad_modulator = mm(all_context.astype(LOW), all_modulation.astype(LOW), TN)
    grad_modulator_bias = jnp.sum(all_modulation, axis=0)
    sums = [jnp.sum(part, axis=0) for part in every[2:]]
    return (
        layer_out,
        latents_grad,
        condition_grad,
        grad_modulator,
        grad_modulator_bias,
        grad_attn_input,
        sums[3].reshape(2, columns),
        grad_attn_output,
        sums[2],
        grad_ffn_input,
        sums[1],
        grad_ffn_output,
        sums[0],
    )


def solution(mesh):
    placed = (
        P("dp", None, None),
        P("dp", "tensor"),
        P("tensor", None),
        P(),
        P(None, None, "tensor"),
        P(None, "tensor"),
        P("tensor", None),
        P(),
        P(None, "tensor"),
        P("tensor"),
        P("tensor", None),
        P(),
        P("dp", None, None),
    )
    return jax.shard_map(
        functools.partial(per_device, mesh.shape["dp"], mesh.shape["tensor"]),
        mesh=mesh,
        in_specs=placed,
        out_specs=(
            P("dp", None, None),
            P("dp", None, None),
            P("dp", "tensor"),
            P("tensor", None),
            P(),
            P(None, None, "tensor"),
            P(None, "tensor"),
            P("tensor", None),
            P(),
            P(None, "tensor"),
            P("tensor"),
            P("tensor", None),
            P(),
        ),
        check_vma=False,
    )
```

```python
import functools

import jax
import jax.numpy as jnp
from jax import lax
from jax.experimental import pallas as pl
from jax.experimental.pallas import tpu as pltpu
from jax.sharding import PartitionSpec as P

HEAD = 64
epsilon = 1e-06
SCALE = HEAD ** (-0.5)
LOW = jnp.bfloat16
FULL = jnp.float32
NN = (((1,), (0,)), ((), ()))
NT = (((1,), (1,)), ((), ()))
TN = (((0,), (0,)), ((), ()))


def mm(left, right, dims=NN):
    return lax.dot_general(left, right, dims, preferred_element_type=FULL)


def norm_parts(values):
    centre = values - jnp.mean(values, axis=-1, keepdims=True)
    inverse = lax.rsqrt(jnp.mean(centre * centre, axis=-1, keepdims=True) + epsilon)
    return (centre * inverse, inverse)


def norm_back(grad, normed, inverse):
    return (
        grad
        - jnp.mean(grad, axis=-1, keepdims=True)
        - normed * jnp.mean(grad * normed, axis=-1, keepdims=True)
    ) * inverse


def softmax_t(keys_t, query_t):
    scores = mm(keys_t, query_t, TN) * SCALE
    shifted = jnp.exp(scores - jnp.max(scores, axis=0, keepdims=True))
    return shifted * (1.0 / jnp.sum(shifted, axis=0, keepdims=True))


def forward_kernel(images, entry_ref, weight_ref, bias_ref, out_ref):
    columns = weight_ref.shape[1]
    positions = entry_ref.shape[0] // images
    entry = entry_ref[...]
    query, keys, values = (
        (mm(weight_ref[j], entry, NT) + bias_ref[j]).astype(LOW) for j in range(3)
    )
    for g in range(images):
        token = slice(g * positions, (g + 1) * positions)
        for h in range(columns // HEAD):
            row = slice(h * HEAD, (h + 1) * HEAD)
            probs = softmax_t(keys[row, token], query[row, token])
            mixed = mm(values[row, token], probs.astype(LOW))
            out_ref[row, token] = mixed.astype(LOW).astype(FULL)


def attention_forward(entry, weight_t, bias, images):
    tokens = entry.shape[0]
    columns = weight_t.shape[1]
    return pl.pallas_call(
        functools.partial(forward_kernel, images),
        out_shape=jax.ShapeDtypeStruct((columns, tokens), FULL),
        compiler_params=pltpu.CompilerParams(vmem_limit_bytes=48 * 2**20),
        name="attention_forward",
    )(entry, weight_t, bias)


def backward_kernel(heads, proj_ref, grad_ref, out_ref):
    for h in range(heads):
        row = slice(h * HEAD, (h + 1) * HEAD)
        query, keys, values = proj_ref[0, row, :], proj_ref[1, row, :], proj_ref[2, row, :]
        grad = grad_ref[row, :]
        probs = softmax_t(keys, query)
        probs_grad = mm(values, grad, TN)
        weighted = probs * probs_grad
        scores_grad = (weighted - probs * jnp.sum(weighted, axis=0, keepdims=True)).astype(LOW)
        out_ref[0, row, :] = (mm(keys, scores_grad) * SCALE).astype(LOW)
        out_ref[1, row, :] = (mm(query, scores_grad, NT) * SCALE).astype(LOW)
        out_ref[2, row, :] = mm(grad, probs.astype(LOW), NT).astype(LOW)


def attention_backward(proj_t, grad_t, images):
    width, tokens = grad_t.shape
    positions = tokens // images
    heads = width // HEAD
    step = 4 if heads % 4 == 0 else heads
    rows = step * HEAD
    return pl.pallas_call(
        functools.partial(backward_kernel, step),
        out_shape=jax.ShapeDtypeStruct((3, width, tokens), LOW),
        grid=(images, heads // step),
        in_specs=[
            pl.BlockSpec((3, rows, positions), lambda g, h: (0, h, g)),
            pl.BlockSpec((rows, positions), lambda g, h: (h, g)),
        ],
        out_specs=pl.BlockSpec((3, rows, positions), lambda g, h: (0, h, g)),
        compiler_params=pltpu.CompilerParams(vmem_limit_bytes=48 * 2**20),
        name="attention_backward",
    )(proj_t, grad_t)


def put_in_order(place_ref, pieces, wide_ref):
    groups, share = place_ref.shape[0] - 1, pieces[0].shape[2]
    rows = wide_ref.shape[0] // groups
    for side in range(2):
        for half in range(2):
            piece = pieces[2 * side + half]
            for spot in range(4):
                first, second = spot % 2, spot // 2
                mask = side + (2 * first + 4 * second if half == 0 else 4 * first + 2 * second)
                share_at = (place_ref[0] ^ mask) * share
                for k in range(2):
                    start = place_ref[1 + 2 * half + k] * rows + share_at
                    wide_ref[pl.ds(pl.multiple_of(start, 8), share), :] = piece[spot, k]


def join_kernel(place_ref, mixed_ref, bias_ref, inputs_ref, mod_ref, *refs):
    pieces, (attention_ref, middle_ref, entry_ref, low_ref, wide_ref) = refs[:-5], refs[-5:]

    @pl.when(pl.program_id(0) == 0)
    def _():
        put_in_order(place_ref, pieces, wide_ref)
        low_ref[...] = wide_ref[...].astype(LOW)

    attention = mm(mixed_ref[...].astype(LOW), low_ref[...], TN) + bias_ref[...].astype(FULL)
    attention_ref[...] = attention
    middle = inputs_ref[...].astype(FULL) + mod_ref[0, 2:3, :] * attention
    middle_ref[...] = middle
    normed = norm_parts(middle)[0]
    entry_ref[...] = (normed * (1.0 + mod_ref[0, 4:5, :]) + mod_ref[0, 3:4, :]).astype(LOW)


def join_heads(places, mixed, pieces, bias, inputs, modulation):
    images = modulation.shape[0]
    tokens, width = inputs.shape
    positions = tokens // images
    rows = mixed.shape[0]
    by_image = pl.BlockSpec((positions, width), lambda g: (g, 0))
    piece = pl.BlockSpec(pieces[0].shape, lambda g: (0, 0, 0, 0))
    return pl.pallas_call(
        join_kernel,
        out_shape=(
            jax.ShapeDtypeStruct((tokens, width), FULL),
            jax.ShapeDtypeStruct((tokens, width), FULL),
            jax.ShapeDtypeStruct((tokens, width), LOW),
            jax.ShapeDtypeStruct((rows, width), LOW),
        ),
        grid=(images,),
        in_specs=[
            pl.BlockSpec(memory_space=pltpu.SMEM),
            pl.BlockSpec((rows, positions), lambda g: (0, g)),
            pl.BlockSpec((1, width), lambda g: (0, 0)),
            by_image,
            pl.BlockSpec((1, 6, width), lambda g: (g, 0, 0)),
        ]
        + [piece] * len(pieces),
        out_specs=(by_image, by_image, by_image, pl.BlockSpec((rows, width), lambda g: (0, 0))),
        scratch_shapes=[pltpu.VMEM((rows, width), FULL)],
        compiler_params=pltpu.CompilerParams(vmem_limit_bytes=48 * 2**20),
        name="join_heads",
    )(places, mixed, bias, inputs, modulation, *pieces)


def project_kernel(place_ref, bias_ref, entry_ref, *refs):
    pieces, (out_ref, low_ref, wide_ref) = refs[:-3], refs[-3:]
    groups = place_ref.shape[0] - 1
    columns = wide_ref.shape[0] // (3 * groups)
    put_in_order(place_ref, pieces, wide_ref)
    entry = entry_ref[...]
    for t in range(groups):
        for j in range(3):
            at = (3 * t + j) * columns
            weight = wide_ref[at : at + columns, :].astype(LOW)
            row = slice(t * columns, (t + 1) * columns)
            low_ref[j, row, :] = weight
            out_ref[j, row, :] = (mm(weight, entry, NT) + bias_ref[j, row]).astype(LOW)


def project_all(pieces, places, bias, entry):
    groups = places.shape[0] - 1
    tokens, width = entry.shape
    vmem = pl.BlockSpec(memory_space=pltpu.VMEM)
    rows = bias.shape[1]
    return pl.pallas_call(
        project_kernel,
        out_shape=(
            jax.ShapeDtypeStruct((3, rows, tokens), LOW),
            jax.ShapeDtypeStruct((3, rows, width), LOW),
        ),
        in_specs=[pl.BlockSpec(memory_space=pltpu.SMEM)] + [vmem] * (2 + len(pieces)),
        out_specs=(vmem, vmem),
        scratch_shapes=[pltpu.VMEM((3 * rows, width), FULL)],
        compiler_params=pltpu.CompilerParams(vmem_limit_bytes=48 * 2**20),
        name="project_all",
    )(places, bias, entry, *pieces)


def middle_kernel(
    grad_ref, middle_ref, attention_ref, upstream_ref, mod_ref, weight_ref,
    middle_grad_ref, low_ref, mixed_grad_ref, sums_ref,
):
    grad = grad_ref[...]
    normed, inverse = norm_parts(middle_ref[...])
    sums_ref[0, 2:3, :] = jnp.sum(grad * normed, axis=0, keepdims=True)
    sums_ref[0, 1:2, :] = jnp.sum(grad, axis=0, keepdims=True)
    middle_grad = upstream_ref[...].astype(FULL)
    middle_grad = middle_grad + norm_back(grad * (1.0 + mod_ref[0, 4:5, :]), normed, inverse)
    middle_grad_ref[...] = middle_grad
    sums_ref[0, 0:1, :] = jnp.sum(middle_grad * attention_ref[...], axis=0, keepdims=True)
    low = (mod_ref[0, 2:3, :] * middle_grad).astype(LOW)
    low_ref[...] = low
    sums_ref[0, 3:4, :] = jnp.sum(low.astype(FULL), axis=0, keepdims=True)
    mixed_grad_ref[...] = mm(weight_ref[...], low, NT).astype(LOW)


def middle_backward(grad, middle, attention, upstream, modulation, weight):
    images = modulation.shape[0]
    tokens, width = grad.shape
    positions = tokens // images
    by_image = pl.BlockSpec((positions, width), lambda g: (g, 0))
    return pl.pallas_call(
        middle_kernel,
        out_shape=(
            jax.ShapeDtypeStruct((tokens, width), FULL),
            jax.ShapeDtypeStruct((tokens, width), LOW),
            jax.ShapeDtypeStruct((weight.shape[0], tokens), LOW),
            jax.ShapeDtypeStruct((images, 4, width), FULL),
        ),
        grid=(images,),
        in_specs=[
            by_image,
            by_image,
            by_image,
            by_image,
            pl.BlockSpec((1, 6, width), lambda g: (g, 0, 0)),
            pl.BlockSpec(weight.shape, lambda g: (0, 0)),
        ],
        out_specs=(
            by_image,
            by_image,
            pl.BlockSpec((weight.shape[0], positions), lambda g: (0, g)),
            pl.BlockSpec((1, 4, width), lambda g: (g, 0, 0)),
        ),
        compiler_params=pltpu.CompilerParams(vmem_limit_bytes=48 * 2**20),
        name="middle_backward",
    )(grad, middle, attention, upstream, modulation, weight)


def entry_kernel(proj_ref, weight_ref, inputs_ref, middle_grad_ref, mod_ref, out_ref, sums_ref):
    grad = mm(proj_ref[...], weight_ref[...], TN)
    normed, inverse = norm_parts(inputs_ref[...].astype(FULL))
    sums_ref[0, 0:1, :] = jnp.sum(grad, axis=0, keepdims=True)
    sums_ref[0, 1:2, :] = jnp.sum(grad * normed, axis=0, keepdims=True)
    back = norm_back(grad * (1.0 + mod_ref[0, 1:2, :]), normed, inverse)
    out_ref[...] = middle_grad_ref[...] + back


def entry_backward(proj_grad, weight, inputs, middle_grad, modulation):
    images = modulation.shape[0]
    tokens, width = inputs.shape
    positions = tokens // images
    by_image = pl.BlockSpec((positions, width), lambda g: (g, 0))
    return pl.pallas_call(
        entry_kernel,
        out_shape=(
            jax.ShapeDtypeStruct((tokens, width), FULL),
            jax.ShapeDtypeStruct((images, 2, width), FULL),
        ),
        grid=(images,),
        in_specs=[
            pl.BlockSpec((proj_grad.shape[0], positions), lambda g: (0, g)),
            pl.BlockSpec(weight.shape, lambda g: (0, 0)),
            by_image,
            by_image,
            pl.BlockSpec((1, 6, width), lambda g: (g, 0, 0)),
        ],
        out_specs=(by_image, pl.BlockSpec((1, 2, width), lambda g: (g, 0, 0))),
        compiler_params=pltpu.CompilerParams(vmem_limit_bytes=48 * 2**20),
        name="entry_backward",
    )(proj_grad, weight, inputs, middle_grad, modulation)


def tie_kernel(*refs):
    pass


def tie(value, *others):
    anywhere = pl.BlockSpec(memory_space=pl.ANY)
    return pl.pallas_call(
        tie_kernel,
        out_shape=jax.ShapeDtypeStruct(value.shape, value.dtype),
        in_specs=[anywhere] * (1 + len(others)),
        out_specs=anywhere,
        input_output_aliases={0: 0},
        name="tie",
    )(value, *others)


def flip(value, axis, count, mask):
    return lax.ppermute(value, axis, [(i, i ^ mask) for i in range(count)])


def flip_sum(value, axis, count):
    parts = [value] + [flip(value, axis, count, mask) for mask in range(1, count)]
    while len(parts) > 1:
        parts = [a + b for a, b in zip(parts[::2], parts[1::2])]
    return parts[0]


def dp_masks(count):
    masks = [1 << i for i in range(count.bit_length() - 1)]
    return masks, masks[:1] + masks[:0:-1]


def halve(value, axis, count, masks):
    place = lax.axis_index(axis)
    for mask in masks:
        half = value.shape[0] // 2
        side = (place // mask) % 2
        away = lax.dynamic_slice_in_dim(value, (1 - side) * half, half, 0)
        kept = lax.dynamic_slice_in_dim(value, side * half, half, 0)
        value = kept + flip(away, axis, count, mask)
    return value


def double(value, axis, count, masks):
    place = lax.axis_index(axis)
    for mask in reversed(masks):
        other = flip(value, axis, count, mask)
        lower = (place // mask) % 2 == 0
        value = jnp.concatenate([jnp.where(lower, value, other), jnp.where(lower, other, value)])
    return value


def gather_z(rows, n_tensor):
    share = rows.shape[0] // 8
    mine = lax.dynamic_slice_in_dim(rows, (lax.axis_index("dp") % 8) * share, share, 0).astype(FULL)
    parts = [mine] + [flip(mine, "tensor", n_tensor, mask) for mask in range(1, n_tensor)]
    return [jnp.stack(parts[:2])[None], jnp.stack(parts[2:])[None]]


def gather_pieces(pieces, n_dp):
    for masks in ((2, 4), (4, 2)):
        moved = [flip(piece, "dp", n_dp, mask) for piece, mask in zip(pieces, masks)]
        pieces = [jnp.concatenate(pair) for pair in zip(pieces, moved)]
    return pieces + [flip(piece, "dp", n_dp, 1) for piece in pieces]


def as_one(function, *operands):
    shapes = jax.eval_shape(function, *operands)
    nothing = lambda *_: jax.tree.map(lambda leaf: jnp.zeros(leaf.shape, leaf.dtype), shapes)
    return lax.cond(lax.axis_index("dp") >= 0, function, nothing, *operands)


def per_device(
    n_dp,
    n_tensor,
    latents,
    condition,
    modulator,
    modulator_bias,
    attn_input,
    attn_input_bias,
    attn_output,
    attn_output_bias,
    ffn_input,
    ffn_input_bias,
    ffn_output,
    ffn_output_bias,
    cotangent,
):
    image_count, positions, features = latents.shape
    tokens = image_count * positions
    columns = attn_input.shape[2]
    place = lax.axis_index("tensor")

    weight_t = attn_input.swapaxes(1, 2)
    places = [lax.axis_index("dp") % 8] + [place ^ mask for mask in range(n_tensor)]
    places = jnp.stack(places).astype(jnp.int32)
    orders = dp_masks(n_dp)
    output_pieces = gather_pieces(gather_z(attn_output, n_tensor), n_dp)
    in_bias = attn_input_bias.astype(FULL)
    bias_own = jnp.stack([in_bias[0], jnp.zeros_like(in_bias[0]), in_bias[1]])
    bias_full = jnp.zeros((3, n_tensor * columns), FULL)
    bias_full = lax.dynamic_update_slice_in_dim(bias_full, bias_own, place * columns, 1)

    cond_float = condition.astype(FULL)
    context_low = jax.nn.silu(cond_float).astype(LOW)
    partial = mm(context_low, modulator)
    shared = jnp.concatenate([partial.reshape(-1), bias_full.reshape(-1)]).reshape(-1, 128)
    shared = flip_sum(shared, "tensor", n_tensor).reshape(-1)
    bias_full = shared[partial.size :].reshape(3, -1, 1)
    modulation = shared[: partial.size].reshape(partial.shape) + modulator_bias.astype(FULL)
    modulation = modulation.reshape(image_count, 6, features)
    pieces = modulation[:, None]
    shift_one, scale_one, gate_two = (pieces[:, :, 0], pieces[:, :, 1], pieces[:, :, 5])
    inputs = latents.astype(FULL)
    normed_one = norm_parts(inputs)[0]
    entry_one = (normed_one * (1.0 + scale_one) + shift_one).astype(LOW).reshape(-1, features)
    mixed_t = attention_forward(entry_one, weight_t, bias_own[:, :, None], image_count)
    mixed_full = jnp.zeros((n_tensor,) + mixed_t.shape, FULL)
    for mask in range(n_tensor):
        part = flip(mixed_t, "tensor", n_tensor, mask) if mask else mixed_t
        mixed_full = lax.dynamic_update_index_in_dim(mixed_full, part, place ^ mask, 0)
    mixed_full = mixed_full.reshape(-1, tokens)
    attention, middle, entry_two, output_full = join_heads(
        places,
        mixed_full,
        output_pieces,
        attn_output_bias[None],
        latents.reshape(-1, features),
        modulation,
    )
    weight_pieces = gather_z(tie(weight_t.reshape(-1, features), mixed_full), n_tensor)
    hidden = mm(entry_two, ffn_input) + ffn_input_bias.astype(FULL)
    active, gelu_pull = jax.vjp(lambda inner: jax.nn.gelu(inner, approximate=True), hidden)
    active = active.astype(LOW)
    upstream = cotangent.astype(FULL)
    branch_grad = (gate_two * upstream).astype(LOW).reshape(-1, features)
    active_grad = mm(branch_grad, ffn_output, NT)
    hidden_grad = gelu_pull(active_grad)[0].astype(LOW)
    entry_two_part = mm(tie(hidden_grad, *weight_pieces), ffn_input, NT)
    entry_two_grad = lax.psum(entry_two_part, "tensor")
    branch_part = mm(active, ffn_output)

    def beside_entry_two(places, first, second, active, branch_grad, entry_two, hidden_grad):
        shares = [mm(active, branch_grad, TN), mm(entry_two, hidden_grad, TN)]
        shares = [halve(x, "dp", n_dp, order) for x, order in zip(shares, orders)]
        weight_pieces = gather_pieces([first, second], n_dp)
        return shares, project_all(weight_pieces, places, bias_full, entry_one)

    shares, (proj_full, weight_full) = as_one(
        beside_entry_two,
        tie(places, entry_two_part),
        *weight_pieces,
        active,
        branch_grad,
        entry_two,
        hidden_grad,
    )
    entry_two_grad = tie(entry_two_grad, proj_full)
    grad_ffn_output_bias = jnp.sum(branch_grad.astype(FULL), axis=0)
    grad_ffn_input_bias = jnp.sum(hidden_grad.astype(FULL), axis=0)


    middle_grad, attention_grad, mixed_grad_t, middle_sums = middle_backward(
        entry_two_grad, middle, attention, cotangent.reshape(-1, features), modulation, output_full
    )
    branch_part = tie(branch_part, mixed_grad_t)
    branch = lax.psum(branch_part, "tensor")

    def beside_branch(mixed_grad_t, proj_full, weight_full, shares, attention_grad, middle_grad):
        ffn_grads = [double(x, "dp", n_dp, order) for x, order in zip(shares, orders)]
        proj_grad = attention_backward(proj_full, mixed_grad_t, image_count)
        own = lax.dynamic_slice_in_dim(proj_grad, place * columns, columns, 1)
        grad_input = mm(own.reshape(-1, tokens), entry_one)
        grad_output = mm(mixed_t.astype(LOW), attention_grad)
        half = 2 * columns
        grads = [grad_input[:half], jnp.concatenate([grad_input[half:], grad_output])]
        grads = [
            double(halve(x, "dp", n_dp, order), "dp", n_dp, order) for x, order in zip(grads, orders)
        ]
        latents_grad, entry_sums = entry_backward(
            proj_grad.reshape(-1, tokens),
            weight_full.reshape(-1, features),
            latents.reshape(-1, features),
            middle_grad,
            modulation,
        )
        own_sums = jnp.sum(own.astype(FULL), axis=2)
        grad_input = jnp.concatenate([grads[0], grads[1][: 3 * columns - half]])
        grad_output = grads[1][3 * columns - half :]
        return ffn_grads, grad_input, grad_output, latents_grad, entry_sums, own_sums

    ffn_grads, grad_attn_input, grad_attn_output, latents_grad, entry_sums, own_sums = as_one(
        beside_branch,
        tie(mixed_grad_t, branch_part),
        proj_full,
        weight_full,
        shares,
        attention_grad,
        middle_grad,
    )
    grad_ffn_output, grad_ffn_input = ffn_grads
    grad_attn_input = grad_attn_input.reshape(3, columns, features).swapaxes(1, 2)
    grad_attn_input_bias = jnp.stack([own_sums[0], own_sums[2]])
    branch = tie(branch, grad_attn_output, latents_grad)
    branch = (branch + ffn_output_bias.astype(FULL)).reshape(latents.shape)
    layer_out = (middle.reshape(latents.shape) + gate_two * branch).astype(LOW)
    gate_two_grad = jnp.sum(upstream * branch, axis=1)
    modulation_grad = jnp.concatenate(
        [
            entry_sums.reshape(image_count, -1),
            middle_sums[:, :3].reshape(image_count, -1),
            gate_two_grad,
        ],
        axis=-1,
    ).astype(LOW)
    grad_attn_output_bias = jnp.sum(middle_sums[:, 3], axis=0)
    context_grad = mm(modulation_grad, modulator, NT)
    condition_grad = jax.vjp(jax.nn.silu, cond_float)[1](context_grad)[0]

    small = jnp.concatenate(
        [
            modulation_grad.astype(FULL).reshape(-1),
            context_low.astype(FULL).reshape(-1),
            grad_ffn_output_bias,
            grad_ffn_input_bias,
            grad_attn_output_bias,
            grad_attn_input_bias.reshape(-1),
        ]
    )
    sizes = [image_count * 6 * features, image_count * condition.shape[1]]
    sizes += [features, ffn_input.shape[1], features, 2 * columns]
    spread = lax.optimization_barrier(lax.all_gather(small, "dp"))
    cuts = [sum(sizes[: i + 1]) for i in range(len(sizes) - 1)]
    every = jnp.split(spread, cuts, axis=1)
    all_modulation = every[0].reshape(-1, 6 * features)
    all_context = every[1].reshape(-1, condition.shape[1])
    grad_modulator = mm(all_context.astype(LOW), all_modulation.astype(LOW), TN)
    grad_modulator_bias = jnp.sum(all_modulation, axis=0)
    sums = [jnp.sum(part, axis=0) for part in every[2:]]
    return (
        layer_out,
        latents_grad.reshape(latents.shape),
        condition_grad,
        grad_modulator,
        grad_modulator_bias,
        grad_attn_input,
        sums[3].reshape(2, columns),
        grad_attn_output,
        sums[2],
        grad_ffn_input,
        sums[1],
        grad_ffn_output,
        sums[0],
    )


def solution(mesh):
    placed = (
        P("dp", None, None),
        P("dp", "tensor"),
        P("tensor", None),
        P(),
        P(None, None, "tensor"),
        P(None, "tensor"),
        P("tensor", None),
        P(),
        P(None, "tensor"),
        P("tensor"),
        P("tensor", None),
        P(),
        P("dp", None, None),
    )
    return jax.shard_map(
        functools.partial(per_device, mesh.shape["dp"], mesh.shape["tensor"]),
        mesh=mesh,
        in_specs=placed,
        out_specs=(
            P("dp", None, None),
            P("dp", None, None),
            P("dp", "tensor"),
            P("tensor", None),
            P(),
            P(None, None, "tensor"),
            P(None, "tensor"),
            P("tensor", None),
            P(),
            P(None, "tensor"),
            P("tensor"),
            P("tensor", None),
            P(),
        ),
        check_vma=False,
    )
```

```python
import functools

import jax
import jax.numpy as jnp
from jax import lax
from jax.experimental import pallas as pl
from jax.experimental.pallas import tpu as pltpu
from jax.sharding import PartitionSpec as P

HEAD = 64
epsilon = 1e-06
SCALE = HEAD ** (-0.5)
LOW = jnp.bfloat16
FULL = jnp.float32
NN = (((1,), (0,)), ((), ()))
NT = (((1,), (1,)), ((), ()))
TN = (((0,), (0,)), ((), ()))
GROUP = 8
CHIPS = 4


def mm(left, right, dims=NN):
    return lax.dot_general(left, right, dims, preferred_element_type=FULL)


def norm_parts(values):
    centre = values - jnp.mean(values, axis=-1, keepdims=True)
    inverse = lax.rsqrt(jnp.mean(centre * centre, axis=-1, keepdims=True) + epsilon)
    return (centre * inverse, inverse)


def norm_back(grad, normed, inverse):
    return (
        grad
        - jnp.mean(grad, axis=-1, keepdims=True)
        - normed * jnp.mean(grad * normed, axis=-1, keepdims=True)
    ) * inverse


def shape(dims, dtype=FULL):
    return jax.ShapeDtypeStruct(dims, dtype)


def rows_at(start, count, step=8):
    return pl.ds(pl.multiple_of(start, step), count)


def call(kernel, name, out_shape, operands, smem=0, grid=None, specs=None, out_specs=None, scratch=()):
    vmem = pl.BlockSpec(memory_space=pltpu.VMEM)
    in_specs = [pl.BlockSpec(memory_space=pltpu.SMEM)] * smem
    in_specs += [vmem] * (len(operands) - smem) if specs is None else specs
    if out_specs is None:
        out_specs = jax.tree.map(lambda _: vmem, out_shape)
    extra = {} if grid is None else {"grid": grid}
    return pl.pallas_call(
        kernel,
        out_shape=out_shape,
        in_specs=in_specs,
        out_specs=out_specs,
        scratch_shapes=list(scratch),
        compiler_params=pltpu.CompilerParams(vmem_limit_bytes=48 * 2**20),
        name=name,
        **extra,
    )(*operands)


def bias_columns(row, count):
    return mm(row, jnp.ones((1, count), LOW), TN)


def softmax_t(keys_t, query_t):
    scores = mm(keys_t, query_t, TN) * SCALE
    shifted = jnp.exp(scores - jnp.max(scores, axis=0, keepdims=True))
    return shifted * (1.0 / jnp.sum(shifted, axis=0, keepdims=True))


def start_kernel(
    part0, part1, part2, part3, mod_bias, latents, weight, bias,
    mixed_ref, entry_ref, mod_ref, bias_ref,
):
    images, _, width = mod_ref.shape
    columns = weight.shape[1]
    positions = latents.shape[0] // images
    shared = (part0[...] + part1[...]) + (part2[...] + part3[...])
    for j in range(3):
        bias_ref[j : j + 1, :] = shared[images : images + 1, j * width : (j + 1) * width]
    modulation = shared[:images] + mod_bias[...].astype(FULL)
    for p in range(6):
        for g in range(images):
            mod_ref[g, p : p + 1, :] = modulation[g : g + 1, p * width : (p + 1) * width]
    offsets = [bias_columns(bias[j : j + 1, :], positions) for j in range(3)]
    for g in range(images):
        token = slice(g * positions, (g + 1) * positions)
        normed = norm_parts(latents[token, :].astype(FULL))[0]
        entry = (normed * (1.0 + mod_ref[g, 1:2, :]) + mod_ref[g, 0:1, :]).astype(LOW)
        entry_ref[token, :] = entry
        query, keys, values = (
            (mm(weight[j], entry, NT) + offsets[j]).astype(LOW) for j in range(3)
        )
        for h in range(columns // HEAD):
            row = slice(h * HEAD, (h + 1) * HEAD)
            probs = softmax_t(keys[row], query[row])
            mixed_ref[row, token] = mm(values[row], probs.astype(LOW)).astype(LOW).astype(FULL)


def probs_kernel(proj_ref, out_ref):
    for h in range(out_ref.shape[1]):
        row = slice(h * HEAD, (h + 1) * HEAD)
        out_ref[0, h] = softmax_t(proj_ref[1, row, :], proj_ref[0, row, :])


def all_probs(proj_t, images):
    _, width, tokens = proj_t.shape
    positions = tokens // images
    heads = width // HEAD
    step = 4 if heads % 4 == 0 else heads
    return call(
        probs_kernel,
        "all_probs",
        shape((images, heads, positions, positions)),
        (proj_t,),
        grid=(images, heads // step),
        specs=[pl.BlockSpec((2, step * HEAD, positions), lambda g, h: (0, h, g))],
        out_specs=pl.BlockSpec((1, step, positions, positions), lambda g, h: (g, h, 0, 0)),
    )


def backward_kernel(probs_ref, proj_ref, grad_ref, out_ref):
    for h in range(probs_ref.shape[1]):
        row = slice(h * HEAD, (h + 1) * HEAD)
        query, keys, values = proj_ref[0, row, :], proj_ref[1, row, :], proj_ref[2, row, :]
        grad = grad_ref[row, :]
        probs = probs_ref[0, h]
        probs_grad = mm(values, grad, TN)
        weighted = probs * probs_grad
        scores_grad = (weighted - probs * jnp.sum(weighted, axis=0, keepdims=True)).astype(LOW)
        out_ref[0, row, :] = (mm(keys, scores_grad) * SCALE).astype(LOW)
        out_ref[1, row, :] = (mm(query, scores_grad, NT) * SCALE).astype(LOW)
        out_ref[2, row, :] = mm(grad, probs.astype(LOW), NT).astype(LOW)


def attention_backward(probs, proj_t, grad_t):
    images, heads, positions, _ = probs.shape
    width, tokens = grad_t.shape
    step = 4 if heads % 4 == 0 else heads
    rows = step * HEAD
    block = pl.BlockSpec((3, rows, positions), lambda g, h: (0, h, g))
    return call(
        backward_kernel,
        "attention_backward",
        shape((3, width, tokens), LOW),
        (probs, proj_t, grad_t),
        grid=(images, heads // step),
        specs=[
            pl.BlockSpec((1, step, positions, positions), lambda g, h: (g, h, 0, 0)),
            block,
            pl.BlockSpec((rows, positions), lambda g, h: (h, g)),
        ],
        out_specs=block,
    )


def put_in_order(place, pieces, wide_ref):
    core, chip, z = place[0], place[1], place[2]
    groups, share, _ = pieces[0].shape
    rows = wide_ref.shape[0] // groups
    for m, piece in enumerate(pieces):
        owner = 2 * (chip ^ (m % CHIPS)) + (core ^ (m // CHIPS))
        for k in range(groups):
            start = (z ^ k) * rows + owner * share
            wide_ref[rows_at(start, share), :] = piece[k]


def join_kernel(place, mixed0, mixed1, mixed2, mixed3, bias, inputs, mod, *refs):
    pieces, (attention_ref, middle_ref, entry_ref, low_ref, wide_ref, mixed_ref) = refs[:-6], refs[-6:]

    @pl.when(pl.program_id(0) == 0)
    def _():
        put_in_order(place, pieces, wide_ref)
        low_ref[...] = wide_ref[...].astype(LOW)

    for k, mixed in enumerate((mixed0, mixed1, mixed2, mixed3)):
        columns = mixed.shape[0]
        mixed_ref[rows_at((place[2] ^ k) * columns, columns, 16), :] = mixed[...].astype(LOW)
    attention = mm(mixed_ref[...], low_ref[...], TN) + bias[...].astype(FULL)
    attention_ref[...] = attention
    middle = inputs[...].astype(FULL) + mod[0, 2:3, :] * attention
    middle_ref[...] = middle
    normed = norm_parts(middle)[0]
    entry_ref[...] = (normed * (1.0 + mod[0, 4:5, :]) + mod[0, 3:4, :]).astype(LOW)


def join_heads(place, mixed, pieces, bias, inputs, modulation):
    images = modulation.shape[0]
    tokens, width = inputs.shape
    positions = tokens // images
    columns = mixed[0].shape[0]
    rows = columns * len(mixed)
    by_image = pl.BlockSpec((positions, width), lambda g: (g, 0))
    specs = [pl.BlockSpec((columns, positions), lambda g: (0, g))] * len(mixed)
    specs += [pl.BlockSpec((1, width), lambda g: (0, 0)), by_image]
    specs += [pl.BlockSpec((1, 6, width), lambda g: (g, 0, 0))]
    specs += [pl.BlockSpec(pieces[0].shape, lambda g: (0, 0, 0))] * len(pieces)
    return call(
        join_kernel,
        "join_heads",
        (
            shape((tokens, width)),
            shape((tokens, width)),
            shape((tokens, width), LOW),
            shape((rows, width), LOW),
        ),
        (place, *mixed, bias, inputs, modulation, *pieces),
        smem=1,
        grid=(images,),
        specs=specs,
        out_specs=(by_image, by_image, by_image, pl.BlockSpec((rows, width), lambda g: (0, 0))),
        scratch=[pltpu.VMEM((rows, width), FULL), pltpu.VMEM((rows, positions), LOW)],
    )


def project_kernel(weight_ref, bias, entry, out_ref, low_ref):
    groups, _, columns, _ = weight_ref.shape
    for j in range(3):
        offsets = bias_columns(bias[j : j + 1, :].astype(LOW), entry.shape[0])
        for t in range(groups):
            weight = weight_ref[t, j].astype(LOW)
            row = slice(t * columns, (t + 1) * columns)
            low_ref[j, row, :] = weight
            out_ref[j, row, :] = (mm(weight, entry[...], NT) + offsets[row]).astype(LOW)


def project_all(weight, bias, entry):
    tokens, width = entry.shape
    rows = bias.shape[1]
    return call(
        project_kernel,
        "project_all",
        (shape((3, rows, tokens), LOW), shape((3, rows, width), LOW)),
        (weight, bias, entry),
    )


def middle_kernel(
    grad_ref, middle_ref, attention_ref, upstream_ref, mod_ref, weight_ref,
    middle_grad_ref, low_ref, mixed_grad_ref, sums_ref,
):
    grad = grad_ref[...]
    normed, inverse = norm_parts(middle_ref[...])
    sums_ref[0, 2:3, :] = jnp.sum(grad * normed, axis=0, keepdims=True)
    sums_ref[0, 1:2, :] = jnp.sum(grad, axis=0, keepdims=True)
    middle_grad = upstream_ref[...].astype(FULL)
    middle_grad = middle_grad + norm_back(grad * (1.0 + mod_ref[0, 4:5, :]), normed, inverse)
    middle_grad_ref[...] = middle_grad
    sums_ref[0, 0:1, :] = jnp.sum(middle_grad * attention_ref[...], axis=0, keepdims=True)
    low = (mod_ref[0, 2:3, :] * middle_grad).astype(LOW)
    low_ref[...] = low
    sums_ref[0, 3:4, :] = jnp.sum(low.astype(FULL), axis=0, keepdims=True)
    mixed_grad_ref[...] = mm(weight_ref[...], low, NT).astype(LOW)


def middle_backward(grad, middle, attention, upstream, modulation, weight):
    images = modulation.shape[0]
    tokens, width = grad.shape
    positions = tokens // images
    by_image = pl.BlockSpec((positions, width), lambda g: (g, 0))
    return call(
        middle_kernel,
        "middle_backward",
        (
            shape((tokens, width)),
            shape((tokens, width), LOW),
            shape((weight.shape[0], tokens), LOW),
            shape((images, 4, width)),
        ),
        (grad, middle, attention, upstream, modulation, weight),
        grid=(images,),
        specs=[by_image] * 4
        + [
            pl.BlockSpec((1, 6, width), lambda g: (g, 0, 0)),
            pl.BlockSpec(weight.shape, lambda g: (0, 0)),
        ],
        out_specs=(
            by_image,
            by_image,
            pl.BlockSpec((weight.shape[0], positions), lambda g: (0, g)),
            pl.BlockSpec((1, 4, width), lambda g: (g, 0, 0)),
        ),
    )


def entry_kernel(proj_ref, weight_ref, inputs_ref, middle_grad_ref, mod_ref, out_ref, sums_ref):
    grad = mm(proj_ref[...], weight_ref[...], TN)
    normed, inverse = norm_parts(inputs_ref[...].astype(FULL))
    sums_ref[0, 0:1, :] = jnp.sum(grad, axis=0, keepdims=True)
    sums_ref[0, 1:2, :] = jnp.sum(grad * normed, axis=0, keepdims=True)
    back = norm_back(grad * (1.0 + mod_ref[0, 1:2, :]), normed, inverse)
    out_ref[...] = middle_grad_ref[...] + back


def entry_backward(proj_grad, weight, inputs, middle_grad, modulation):
    images = modulation.shape[0]
    tokens, width = inputs.shape
    positions = tokens // images
    by_image = pl.BlockSpec((positions, width), lambda g: (g, 0))
    return call(
        entry_kernel,
        "entry_backward",
        (shape((tokens, width)), shape((images, 2, width))),
        (proj_grad, weight, inputs, middle_grad, modulation),
        grid=(images,),
        specs=[
            pl.BlockSpec((proj_grad.shape[0], positions), lambda g: (0, g)),
            pl.BlockSpec(weight.shape, lambda g: (0, 0)),
            by_image,
            by_image,
            pl.BlockSpec((1, 6, width), lambda g: (g, 0, 0)),
        ],
        out_specs=(by_image, pl.BlockSpec((1, 2, width), lambda g: (g, 0, 0))),
    )


def end_kernel(branch_ref, bias_ref, middle_ref, upstream_ref, mod_ref, out_ref, sums_ref):
    branch = branch_ref[...] + bias_ref[...].astype(FULL)
    out_ref[...] = (middle_ref[...] + mod_ref[0, 5:6, :] * branch).astype(LOW)
    sums_ref[0] = jnp.sum(upstream_ref[...].astype(FULL) * branch, axis=0, keepdims=True)


def end_forward(branch, bias, middle, upstream, modulation):
    images = modulation.shape[0]
    tokens, width = middle.shape
    by_image = pl.BlockSpec((tokens // images, width), lambda g: (g, 0))
    return call(
        end_kernel,
        "end_forward",
        (shape((tokens, width), LOW), shape((images, 1, width))),
        (branch, bias, middle, upstream, modulation),
        grid=(images,),
        specs=[
            by_image,
            pl.BlockSpec((1, width), lambda g: (0, 0)),
            by_image,
            by_image,
            pl.BlockSpec((1, 6, width), lambda g: (g, 0, 0)),
        ],
        out_specs=(by_image, pl.BlockSpec((1, 1, width), lambda g: (g, 0, 0))),
    )


def modulator_kernel(every_ref, context_ref, out_ref, sums_ref):
    part = every_ref[...]
    sums_ref[...] = jnp.sum(part, axis=0, keepdims=True)
    out_ref[...] = mm(context_ref[...].astype(LOW), part.astype(LOW), TN)


def modulator_backward(every, context, width):
    images = every.shape[0]
    total = every.shape[1]
    rows = context.shape[1]
    return call(
        modulator_kernel,
        "modulator_backward",
        (shape((rows, total)), shape((1, total))),
        (every, context),
        grid=(total // width,),
        specs=[
            pl.BlockSpec((images, width), lambda p: (0, p)),
            pl.BlockSpec((images, rows), lambda p: (0, 0)),
        ],
        out_specs=(
            pl.BlockSpec((rows, width), lambda p: (0, p)),
            pl.BlockSpec((1, width), lambda p: (0, p)),
        ),
    )


def mlp_grads_kernel(place, active, branch_grad, entry, hidden_grad, away_ref, kept_ref):
    half = active.shape[1] // 2
    for ref, core in ((away_ref, 1 - place[0]), (kept_ref, place[0])):
        column = rows_at(core * half, half, 128)
        ref[:half, :] = mm(active[:, column], branch_grad[...], TN)
        ref[half:, :] = mm(entry[:, column], hidden_grad[...], TN)


def mlp_grads(place, active, branch_grad, entry, hidden_grad):
    width = entry.shape[1]
    half = shape((width, width))
    operands = (place, active, branch_grad, entry, hidden_grad)
    return call(mlp_grads_kernel, "mlp_grads", (half, half), operands, smem=1)


def attn_grads_kernel(place, proj, entry, mixed, grad, away_ref, kept_ref, sums_ref, own_ref):
    columns = mixed.shape[0]
    for j in range(3):
        own_ref[j * columns : (j + 1) * columns, :] = proj[j, rows_at(place[2] * columns, columns, 16), :]
    sums_ref[...] = mm(jnp.ones((8, own_ref.shape[1]), LOW), own_ref[...], NT)
    inner, outer = 3 * columns // 2, columns // 2
    for ref, core in ((away_ref, 1 - place[0]), (kept_ref, place[0])):
        ref[:inner, :] = mm(own_ref[rows_at(core * inner, inner, 16), :], entry[...])
        ref[inner:, :] = mm(mixed[rows_at(core * outer, outer), :].astype(LOW), grad[...])


def attn_grads(place, proj, entry, mixed, grad):
    columns, tokens = mixed.shape
    width = entry.shape[1]
    half = shape((2 * columns, width))
    return call(
        attn_grads_kernel,
        "attn_grads",
        (half, half, shape((8, 3 * columns))),
        (place, proj, entry, mixed, grad),
        smem=1,
        scratch=[pltpu.VMEM((3 * columns, tokens), LOW)],
    )


def cut_kernel(shares, place, kept, other, *outs):
    for k, out in enumerate(outs):
        base, at = 0, 0
        for share in shares:
            row = rows_at(base + (place[1] ^ k) * share, share)
            out[at : at + share, :] = kept[row, :] + other[row, :]
            base, at = base + CHIPS * share, at + share


def place_kernel(shares, place, *refs):
    parts, out = refs[:-1], refs[-1]
    for k, part in enumerate(parts):
        base, at = 0, 0
        for share in shares:
            out[rows_at(base + (place[1] ^ k) * share, share), :] = part[at : at + share, :]
            base, at = base + CHIPS * share, at + share


def whole_kernel(shares, place, mine, other, *outs):
    base = 0
    for share, out in zip(shares, outs):
        half = CHIPS * share
        out[rows_at(place[0] * half, half), :] = mine[base : base + half, :]
        out[rows_at((1 - place[0]) * half, half), :] = other[base : base + half, :]
        base += half


def flip(value, axis, count, mask):
    return lax.ppermute(value, axis, [(i, i ^ mask) for i in range(count)])


def sum_shares(place, away, kept, shares, n_dp, *others):
    other = flip(away, "dp", n_dp, 1)
    part = shape((sum(shares), kept.shape[1]))
    parts = call(
        functools.partial(cut_kernel, shares), "cut", (part,) * CHIPS, (place, kept, other), smem=1
    )
    moved = [flip(parts[k], "dp", n_dp, 2 * k) for k in range(1, CHIPS)]
    total = (tie(parts[0], *others) if others else parts[0]) + moved[0] + moved[1] + moved[2]
    masks = [1 << i for i in range(3, n_dp.bit_length() - 1)]
    return double(halve(total, n_dp, masks), n_dp, masks)


def spread_chips(share, n_dp):
    return [share] + [flip(share, "dp", n_dp, 2 * k) for k in range(1, CHIPS)]


def spread_shares(place, parts, shares, n_dp):
    width = parts[0].shape[1]
    half = shape((CHIPS * sum(shares), width))
    mine = call(functools.partial(place_kernel, shares), "place", half, (place, *parts), smem=1)
    other = flip(mine, "dp", n_dp, 1)
    outs = tuple(shape((GROUP * count, width)) for count in shares)
    return call(
        functools.partial(whole_kernel, shares), "whole", outs, (place, mine, other), smem=1
    )


def halve(value, count, masks):
    index = lax.axis_index("dp")
    for mask in masks:
        half = value.shape[0] // 2
        side = (index // mask) % 2
        away = lax.dynamic_slice_in_dim(value, (1 - side) * half, half, 0)
        kept = lax.dynamic_slice_in_dim(value, side * half, half, 0)
        value = kept + flip(away, "dp", count, mask)
    return value


def double(value, count, masks):
    index = lax.axis_index("dp")
    for mask in reversed(masks):
        other = flip(value, "dp", count, mask)
        lower = (index // mask) % 2 == 0
        value = jnp.concatenate([jnp.where(lower, value, other), jnp.where(lower, other, value)])
    return value


def gather_rows(rows, n_dp):
    share = rows.shape[0] // n_dp
    mine = lax.dynamic_slice_in_dim(rows, lax.axis_index("dp") * share, share, 0)
    return lax.all_gather(mine.astype(FULL), ("tensor", "dp"), tiled=True)


def gather_z(rows, n_tensor):
    share = rows.shape[0] // GROUP
    start = (lax.axis_index("dp") % GROUP) * share
    mine = lax.dynamic_slice_in_dim(rows, start, share, 0).astype(FULL)
    return [mine] + [flip(mine, "tensor", n_tensor, k) for k in range(1, n_tensor)]


def gather_pieces(parts, n_dp):
    stacked = jnp.stack(parts)
    pieces = [stacked] + [flip(stacked, "dp", n_dp, 2 * k) for k in range(1, CHIPS)]
    return pieces + [flip(piece, "dp", n_dp, 1) for piece in pieces]


def tie_kernel(*refs):
    pass


def tie(value, *others):
    anywhere = pl.BlockSpec(memory_space=pl.ANY)
    return pl.pallas_call(
        tie_kernel,
        out_shape=jax.ShapeDtypeStruct(value.shape, value.dtype),
        in_specs=[anywhere] * (1 + len(others)),
        out_specs=anywhere,
        input_output_aliases={0: 0},
        name="tie",
    )(value, *others)


def as_one(function, *operands):
    shapes = jax.eval_shape(function, *operands)
    nothing = lambda *_: jax.tree.map(lambda leaf: jnp.zeros(leaf.shape, leaf.dtype), shapes)
    return lax.cond(lax.axis_index("dp") >= 0, function, nothing, *operands)


def per_device(
    n_dp,
    n_tensor,
    latents,
    condition,
    modulator,
    modulator_bias,
    attn_input,
    attn_input_bias,
    attn_output,
    attn_output_bias,
    ffn_input,
    ffn_input_bias,
    ffn_output,
    ffn_output_bias,
    cotangent,
):
    image_count, positions, features = latents.shape
    tokens = image_count * positions
    columns = attn_input.shape[2]
    z = lax.axis_index("tensor")
    member = lax.axis_index("dp") % GROUP
    place = jnp.stack([member % 2, member // 2, z]).astype(jnp.int32)
    inputs = latents.reshape(tokens, features)
    upstream = cotangent.reshape(tokens, features)
    weight_t = attn_input.swapaxes(1, 2)

    weight_wide = gather_rows(weight_t.reshape(-1, features), n_dp)
    weight_wide = weight_wide.reshape(n_tensor, 3, columns, features)
    cond_float = condition.astype(FULL)
    context_low = jax.nn.silu(cond_float).astype(LOW)

    def forward(context_low):
        def start(context_low):
            partial = mm(context_low, modulator)
            bias_own = jnp.stack(
                [attn_input_bias[0], jnp.zeros_like(attn_input_bias[0]), attn_input_bias[1]]
            )
            bias_row = jnp.zeros((3, n_tensor * columns), FULL)
            bias_row = lax.dynamic_update_slice_in_dim(bias_row, bias_own.astype(FULL), z * columns, 1)
            bias_row = bias_row.reshape(1, -1)
            bias_row = jnp.pad(bias_row, ((0, 0), (0, partial.shape[1] - bias_row.shape[1])))
            shared = jnp.concatenate([partial, bias_row])
            shared = [shared] + [flip(shared, "tensor", n_tensor, k) for k in range(1, n_tensor)]
            return call(
                start_kernel,
                "start",
                (
                    shape((columns, tokens)),
                    shape((tokens, features), LOW),
                    shape((image_count, 6, features)),
                    shape((3, n_tensor * columns)),
                ),
                (*shared, modulator_bias[None], inputs, weight_t, bias_own),
            )

        output_parts = gather_z(attn_output, n_tensor)
        mixed_t, entry_one, modulation, bias_full = start(context_low)
        mixed = [mixed_t] + [flip(mixed_t, "tensor", n_tensor, k) for k in range(1, n_tensor)]
        output_pieces = gather_pieces(output_parts, n_dp)
        attention, middle, entry_two, output_full = join_heads(
            place, mixed, output_pieces, attn_output_bias[None], inputs, modulation
        )
        hidden = mm(entry_two, ffn_input) + ffn_input_bias.astype(FULL)
        active, gelu_pull = jax.vjp(lambda inner: jax.nn.gelu(inner, approximate=True), hidden)
        active = active.astype(LOW)
        gate_two = modulation[:, None, 5]
        branch_grad = (gate_two * cotangent.astype(FULL)).astype(LOW).reshape(tokens, features)
        hidden_grad = gelu_pull(mm(branch_grad, ffn_output, NT))[0].astype(LOW)
        part = mm(hidden_grad, ffn_input, NT)
        first = mixed_t, entry_one, modulation, bias_full, attention, middle, output_full
        return first, (active, branch_grad, entry_two, hidden_grad), part

    first, mlp, part = as_one(forward, context_low)
    mixed_t, entry_one, modulation, bias_full, attention, middle, output_full = first
    entry_two_grad = lax.psum(part, "tensor")
    mlp_shares = (ffn_output.shape[0] // GROUP, features // GROUP)

    def beside_entry_two(place, weight_wide, mlp):
        active, branch_grad, entry_two, hidden_grad = mlp
        away, kept = mlp_grads(place, active, branch_grad, entry_two, hidden_grad)
        share = sum_shares(place, away, kept, mlp_shares, n_dp)
        proj_full, weight_full = project_all(weight_wide, bias_full, entry_one)
        mlp_parts = spread_chips(share, n_dp)
        probs = all_probs(proj_full, image_count)
        branch_part = mm(active, ffn_output)
        sums = [jnp.sum(x.astype(FULL), axis=0) for x in (branch_grad, hidden_grad)]
        return mlp_parts, probs, proj_full, weight_full, branch_part, sums

    mlp_parts, probs, proj_full, weight_full, branch_part, mlp_sums = as_one(
        beside_entry_two, tie(place, part), weight_wide, mlp
    )
    entry_two_grad = tie(entry_two_grad, branch_part)
    branch_part = tie(branch_part, entry_two_grad)
    branch = lax.psum(branch_part, "tensor")
    attn_shares = (3 * columns // GROUP, columns // GROUP)

    def beside_branch(entry_two_grad, probs, proj_full, weight_full, mlp_parts):
        def heads(entry_two_grad, probs, proj_full):
            middle_grad, attention_grad, mixed_grad_t, middle_sums = middle_backward(
                entry_two_grad, middle, attention, upstream, modulation, output_full
            )
            proj_grad = attention_backward(probs, proj_full, mixed_grad_t)
            parts = attn_grads(place, proj_grad, entry_one, mixed_t, attention_grad)
            return middle_grad, middle_sums, proj_grad, parts

        middle_grad, middle_sums, proj_grad, (away, kept, own_sums) = as_one(
            heads, entry_two_grad, probs, proj_full
        )
        latents_grad, entry_sums = entry_backward(
            proj_grad.reshape(-1, tokens),
            weight_full.reshape(-1, features),
            inputs,
            middle_grad,
            modulation,
        )
        attn_share = sum_shares(place, away, kept, attn_shares, n_dp, latents_grad)
        mlp_whole = spread_shares(place, mlp_parts, mlp_shares, n_dp)
        attn_parts = spread_chips(attn_share, n_dp)
        attn_parts[0] = tie(attn_parts[0], *mlp_whole)
        attn_whole = spread_shares(place, attn_parts, attn_shares, n_dp)
        return mlp_whole, attn_whole, latents_grad, entry_sums, own_sums, middle_sums

    mlp_whole, attn_whole, latents_grad, entry_sums, own_sums, middle_sums = as_one(
        beside_branch, tie(entry_two_grad, branch_part), probs, proj_full, weight_full, mlp_parts
    )
    layer_out, gate_two_grad = end_forward(
        tie(branch, entry_sums), ffn_output_bias[None], middle, upstream, modulation
    )
    modulation_grad = jnp.concatenate([entry_sums, middle_sums[:, :3], gate_two_grad], axis=1)
    modulation_grad = modulation_grad.reshape(image_count, -1).astype(LOW)
    context_grad = mm(modulation_grad, modulator, NT)
    condition_grad = jax.vjp(jax.nn.silu, cond_float)[1](context_grad)[0]

    sums = [mlp_sums[0], mlp_sums[1], jnp.sum(middle_sums[:, 3], axis=0), own_sums[0]]
    sizes = [part.shape[0] for part in sums]
    sums = jnp.pad(jnp.concatenate(sums)[None], ((0, image_count - 1), (0, 0)))
    small = [modulation_grad.astype(FULL), sums, context_low.astype(FULL)]
    every = lax.all_gather(jnp.concatenate(small, axis=1), "dp", tiled=True)
    every_rows = 6 * features
    context_at = every_rows + sum(sizes)
    grad_modulator, grad_modulator_bias = modulator_backward(
        every[:, :every_rows], every[:, context_at:], features
    )
    sums = jnp.split(jnp.sum(every[:, every_rows:context_at], axis=0), [sum(sizes[:i]) for i in (1, 2, 3)])
    input_bias = sums[3].reshape(3, columns)
    return (
        layer_out.reshape(latents.shape),
        latents_grad.reshape(latents.shape),
        condition_grad,
        grad_modulator,
        grad_modulator_bias[0],
        attn_whole[0].reshape(3, columns, features).swapaxes(1, 2),
        jnp.stack([input_bias[0], input_bias[2]]),
        attn_whole[1],
        sums[2],
        mlp_whole[1],
        sums[1],
        mlp_whole[0],
        sums[0],
    )


def solution(mesh):
    placed = (
        P("dp", None, None),
        P("dp", "tensor"),
        P("tensor", None),
        P(),
        P(None, None, "tensor"),
        P(None, "tensor"),
        P("tensor", None),
        P(),
        P(None, "tensor"),
        P("tensor"),
        P("tensor", None),
        P(),
        P("dp", None, None),
    )
    return jax.shard_map(
        functools.partial(per_device, mesh.shape["dp"], mesh.shape["tensor"]),
        mesh=mesh,
        in_specs=placed,
        out_specs=(
            P("dp", None, None),
            P("dp", None, None),
            P("dp", "tensor"),
            P("tensor", None),
            P(),
            P(None, None, "tensor"),
            P(None, "tensor"),
            P("tensor", None),
            P(),
            P(None, "tensor"),
            P("tensor"),
            P("tensor", None),
            P(),
        ),
        check_vma=False,
    )
```

```python
import functools

import jax
import jax.numpy as jnp
from jax import lax
from jax.experimental import pallas as pl
from jax.experimental.pallas import tpu as pltpu
from jax.sharding import PartitionSpec as P

HEAD = 64
epsilon = 1e-06
SCALE = HEAD ** (-0.5)
LOW = jnp.bfloat16
FULL = jnp.float32
NN = (((1,), (0,)), ((), ()))
NT = (((1,), (1,)), ((), ()))
TN = (((0,), (0,)), ((), ()))
GROUP = 8
CHIPS = 4


def mm(left, right, dims=NN):
    return lax.dot_general(left, right, dims, preferred_element_type=FULL)


def norm_parts(values):
    centre = values - jnp.mean(values, axis=-1, keepdims=True)
    inverse = lax.rsqrt(jnp.mean(centre * centre, axis=-1, keepdims=True) + epsilon)
    return (centre * inverse, inverse)


def norm_back(grad, normed, inverse):
    return (
        grad
        - jnp.mean(grad, axis=-1, keepdims=True)
        - normed * jnp.mean(grad * normed, axis=-1, keepdims=True)
    ) * inverse


def shape(dims, dtype=FULL):
    return jax.ShapeDtypeStruct(dims, dtype)


def rows_at(start, count, step=8):
    return pl.ds(pl.multiple_of(start, step), count)


def call(kernel, name, out_shape, operands, smem=0, grid=None, specs=None, out_specs=None, scratch=()):
    vmem = pl.BlockSpec(memory_space=pltpu.VMEM)
    in_specs = [pl.BlockSpec(memory_space=pltpu.SMEM)] * smem
    in_specs += [vmem] * (len(operands) - smem) if specs is None else specs
    if out_specs is None:
        out_specs = jax.tree.map(lambda _: vmem, out_shape)
    extra = {} if grid is None else {"grid": grid}
    return pl.pallas_call(
        kernel,
        out_shape=out_shape,
        in_specs=in_specs,
        out_specs=out_specs,
        scratch_shapes=list(scratch),
        compiler_params=pltpu.CompilerParams(vmem_limit_bytes=48 * 2**20),
        name=name,
        **extra,
    )(*operands)


def bias_columns(row, count):
    return mm(row, jnp.ones((1, count), LOW), TN)


def softmax_t(keys_t, query_t):
    scores = mm(keys_t, query_t, TN) * SCALE
    shifted = jnp.exp(scores - jnp.max(scores, axis=0, keepdims=True))
    return shifted * (1.0 / jnp.sum(shifted, axis=0, keepdims=True))


def start_kernel(
    part0, part1, part2, part3, mod_bias, latents, weight, bias,
    mixed_ref, entry_ref, mod_ref, bias_ref,
):
    images, _, width = mod_ref.shape
    columns = weight.shape[1]
    positions = latents.shape[0] // images
    shared = (part0[...] + part1[...]) + (part2[...] + part3[...])
    for j in range(3):
        bias_ref[j : j + 1, :] = shared[images : images + 1, j * width : (j + 1) * width]
    modulation = shared[:images] + mod_bias[...].astype(FULL)
    for p in range(6):
        for g in range(images):
            mod_ref[g, p : p + 1, :] = modulation[g : g + 1, p * width : (p + 1) * width]
    offsets = [bias_columns(bias[j : j + 1, :], positions) for j in range(3)]
    for g in range(images):
        token = slice(g * positions, (g + 1) * positions)
        normed = norm_parts(latents[token, :].astype(FULL))[0]
        entry = (normed * (1.0 + mod_ref[g, 1:2, :]) + mod_ref[g, 0:1, :]).astype(LOW)
        entry_ref[token, :] = entry
        query, keys, values = (
            (mm(weight[j], entry, NT) + offsets[j]).astype(LOW) for j in range(3)
        )
        for h in range(columns // HEAD):
            row = slice(h * HEAD, (h + 1) * HEAD)
            probs = softmax_t(keys[row], query[row])
            mixed_ref[row, token] = mm(values[row], probs.astype(LOW)).astype(LOW).astype(FULL)


def probs_kernel(proj_ref, out_ref):
    for h in range(out_ref.shape[1]):
        row = slice(h * HEAD, (h + 1) * HEAD)
        out_ref[0, h] = softmax_t(proj_ref[1, row, :], proj_ref[0, row, :])


def all_probs(proj_t, images):
    _, width, tokens = proj_t.shape
    positions = tokens // images
    heads = width // HEAD
    step = 4 if heads % 4 == 0 else heads
    return call(
        probs_kernel,
        "all_probs",
        shape((images, heads, positions, positions)),
        (proj_t,),
        grid=(images, heads // step),
        specs=[pl.BlockSpec((2, step * HEAD, positions), lambda g, h: (0, h, g))],
        out_specs=pl.BlockSpec((1, step, positions, positions), lambda g, h: (g, h, 0, 0)),
    )


def backward_kernel(probs_ref, proj_ref, grad_ref, out_ref):
    for h in range(probs_ref.shape[1]):
        row = slice(h * HEAD, (h + 1) * HEAD)
        query, keys, values = proj_ref[0, row, :], proj_ref[1, row, :], proj_ref[2, row, :]
        grad = grad_ref[row, :]
        probs = probs_ref[0, h]
        probs_grad = mm(values, grad, TN)
        weighted = probs * probs_grad
        scores_grad = (weighted - probs * jnp.sum(weighted, axis=0, keepdims=True)).astype(LOW)
        out_ref[0, row, :] = (mm(keys, scores_grad) * SCALE).astype(LOW)
        out_ref[1, row, :] = (mm(query, scores_grad, NT) * SCALE).astype(LOW)
        out_ref[2, row, :] = mm(grad, probs.astype(LOW), NT).astype(LOW)


def attention_backward(probs, proj_t, grad_t):
    images, heads, positions, _ = probs.shape
    width, tokens = grad_t.shape
    step = 4 if heads % 4 == 0 else heads
    rows = step * HEAD
    block = pl.BlockSpec((3, rows, positions), lambda g, h: (0, h, g))
    return call(
        backward_kernel,
        "attention_backward",
        shape((3, width, tokens), LOW),
        (probs, proj_t, grad_t),
        grid=(images, heads // step),
        specs=[
            pl.BlockSpec((1, step, positions, positions), lambda g, h: (g, h, 0, 0)),
            block,
            pl.BlockSpec((rows, positions), lambda g, h: (h, g)),
        ],
        out_specs=block,
    )


def put_in_order(place, pieces, wide_ref):
    core, chip, z = place[0], place[1], place[2]
    groups, share, _ = pieces[0].shape
    rows = wide_ref.shape[0] // groups
    for m, piece in enumerate(pieces):
        owner = 2 * (chip ^ (m % CHIPS)) + (core ^ (m // CHIPS))
        for k in range(groups):
            start = (z ^ k) * rows + owner * share
            wide_ref[rows_at(start, share), :] = piece[k]


def join_kernel(place, mixed0, mixed1, mixed2, inner, outer, bias, inputs, mod, *refs):
    pieces, (attention_ref, middle_ref, entry_ref, low_ref, wide_ref, mixed_ref) = refs[:-6], refs[-6:]

    @pl.when(pl.program_id(0) == 0)
    def _():
        put_in_order(place, pieces, wide_ref)
        low_ref[...] = wide_ref[...].astype(LOW)

    mixed = (mixed0[...], mixed1[...], mixed2[...], inner[...] + outer[...])
    for k, part in enumerate(mixed):
        columns = part.shape[0]
        mixed_ref[rows_at((place[2] ^ k) * columns, columns, 16), :] = part.astype(LOW)
    attention = mm(mixed_ref[...], low_ref[...], TN) + bias[...].astype(FULL)
    attention_ref[...] = attention
    middle = inputs[...].astype(FULL) + mod[0, 2:3, :] * attention
    middle_ref[...] = middle
    normed = norm_parts(middle)[0]
    entry_ref[...] = (normed * (1.0 + mod[0, 4:5, :]) + mod[0, 3:4, :]).astype(LOW)


def join_heads(place, mixed, pieces, bias, inputs, modulation):
    images = modulation.shape[0]
    tokens, width = inputs.shape
    positions = tokens // images
    columns = mixed[0].shape[0]
    rows = columns * (len(mixed) - 1)
    by_image = pl.BlockSpec((positions, width), lambda g: (g, 0))
    specs = [pl.BlockSpec((columns, positions), lambda g: (0, g))] * len(mixed)
    specs += [pl.BlockSpec((1, width), lambda g: (0, 0)), by_image]
    specs += [pl.BlockSpec((1, 6, width), lambda g: (g, 0, 0))]
    specs += [pl.BlockSpec(pieces[0].shape, lambda g: (0, 0, 0))] * len(pieces)
    return call(
        join_kernel,
        "join_heads",
        (
            shape((tokens, width)),
            shape((tokens, width)),
            shape((tokens, width), LOW),
            shape((rows, width), LOW),
        ),
        (place, *mixed, bias, inputs, modulation, *pieces),
        smem=1,
        grid=(images,),
        specs=specs,
        out_specs=(by_image, by_image, by_image, pl.BlockSpec((rows, width), lambda g: (0, 0))),
        scratch=[pltpu.VMEM((rows, width), FULL), pltpu.VMEM((rows, positions), LOW)],
    )


def project_kernel(weight_ref, bias, entry, out_ref, low_ref):
    groups, _, columns, _ = weight_ref.shape
    for j in range(3):
        offsets = bias_columns(bias[j : j + 1, :].astype(LOW), entry.shape[0])
        for t in range(groups):
            weight = weight_ref[t, j].astype(LOW)
            row = slice(t * columns, (t + 1) * columns)
            low_ref[j, row, :] = weight
            out_ref[j, row, :] = (mm(weight, entry[...], NT) + offsets[row]).astype(LOW)


def project_all(weight, bias, entry):
    tokens, width = entry.shape
    rows = bias.shape[1]
    return call(
        project_kernel,
        "project_all",
        (shape((3, rows, tokens), LOW), shape((3, rows, width), LOW)),
        (weight, bias, entry),
    )


def middle_kernel(
    grad_ref, middle_ref, attention_ref, upstream_ref, mod_ref, weight_ref,
    middle_grad_ref, low_ref, mixed_grad_ref, sums_ref,
):
    grad = grad_ref[...]
    normed, inverse = norm_parts(middle_ref[...])
    sums_ref[0, 2:3, :] = jnp.sum(grad * normed, axis=0, keepdims=True)
    sums_ref[0, 1:2, :] = jnp.sum(grad, axis=0, keepdims=True)
    middle_grad = upstream_ref[...].astype(FULL)
    middle_grad = middle_grad + norm_back(grad * (1.0 + mod_ref[0, 4:5, :]), normed, inverse)
    middle_grad_ref[...] = middle_grad
    sums_ref[0, 0:1, :] = jnp.sum(middle_grad * attention_ref[...], axis=0, keepdims=True)
    low = (mod_ref[0, 2:3, :] * middle_grad).astype(LOW)
    low_ref[...] = low
    sums_ref[0, 3:4, :] = jnp.sum(low.astype(FULL), axis=0, keepdims=True)
    mixed_grad_ref[...] = mm(weight_ref[...], low, NT).astype(LOW)


def middle_backward(grad, middle, attention, upstream, modulation, weight):
    images = modulation.shape[0]
    tokens, width = grad.shape
    positions = tokens // images
    by_image = pl.BlockSpec((positions, width), lambda g: (g, 0))
    return call(
        middle_kernel,
        "middle_backward",
        (
            shape((tokens, width)),
            shape((tokens, width), LOW),
            shape((weight.shape[0], tokens), LOW),
            shape((images, 4, width)),
        ),
        (grad, middle, attention, upstream, modulation, weight),
        grid=(images,),
        specs=[by_image] * 4
        + [
            pl.BlockSpec((1, 6, width), lambda g: (g, 0, 0)),
            pl.BlockSpec(weight.shape, lambda g: (0, 0)),
        ],
        out_specs=(
            by_image,
            by_image,
            pl.BlockSpec((weight.shape[0], positions), lambda g: (0, g)),
            pl.BlockSpec((1, 4, width), lambda g: (g, 0, 0)),
        ),
    )


def entry_kernel(proj_ref, weight_ref, inputs_ref, middle_grad_ref, mod_ref, out_ref, sums_ref):
    grad = mm(proj_ref[...], weight_ref[...], TN)
    normed, inverse = norm_parts(inputs_ref[...].astype(FULL))
    sums_ref[0, 0:1, :] = jnp.sum(grad, axis=0, keepdims=True)
    sums_ref[0, 1:2, :] = jnp.sum(grad * normed, axis=0, keepdims=True)
    back = norm_back(grad * (1.0 + mod_ref[0, 1:2, :]), normed, inverse)
    out_ref[...] = middle_grad_ref[...] + back


def entry_backward(proj_grad, weight, inputs, middle_grad, modulation):
    images = modulation.shape[0]
    tokens, width = inputs.shape
    positions = tokens // images
    by_image = pl.BlockSpec((positions, width), lambda g: (g, 0))
    return call(
        entry_kernel,
        "entry_backward",
        (shape((tokens, width)), shape((images, 2, width))),
        (proj_grad, weight, inputs, middle_grad, modulation),
        grid=(images,),
        specs=[
            pl.BlockSpec((proj_grad.shape[0], positions), lambda g: (0, g)),
            pl.BlockSpec(weight.shape, lambda g: (0, 0)),
            by_image,
            by_image,
            pl.BlockSpec((1, 6, width), lambda g: (g, 0, 0)),
        ],
        out_specs=(by_image, pl.BlockSpec((1, 2, width), lambda g: (g, 0, 0))),
    )


def end_kernel(branch_ref, bias_ref, middle_ref, mod_ref, out_ref):
    branch = branch_ref[...] + bias_ref[...].astype(FULL)
    out_ref[...] = (middle_ref[...] + mod_ref[0, 5:6, :] * branch).astype(LOW)


def end_forward(branch, bias, middle, modulation):
    images = modulation.shape[0]
    tokens, width = middle.shape
    by_image = pl.BlockSpec((tokens // images, width), lambda g: (g, 0))
    return call(
        end_kernel,
        "end_forward",
        shape((tokens, width), LOW),
        (branch, bias, middle, modulation),
        grid=(images,),
        specs=[
            by_image,
            pl.BlockSpec((1, width), lambda g: (0, 0)),
            by_image,
            pl.BlockSpec((1, 6, width), lambda g: (g, 0, 0)),
        ],
        out_specs=by_image,
    )


def modulator_kernel(every_ref, context_ref, out_ref, sums_ref):
    part = every_ref[...]
    sums_ref[...] = jnp.sum(part, axis=0, keepdims=True)
    context = context_ref[:, : out_ref.shape[0]].astype(LOW)
    out_ref[...] = mm(context, part.astype(LOW), TN)


def modulator_backward(every, rows, context_width, width):
    images = every.shape[0]
    at = 6 * width // context_width
    return call(
        modulator_kernel,
        "modulator_backward",
        (shape((rows, 6 * width)), shape((1, 6 * width))),
        (every, every),
        grid=(6,),
        specs=[
            pl.BlockSpec((images, width), lambda p: (0, p)),
            pl.BlockSpec((images, context_width), lambda p: (0, at)),
        ],
        out_specs=(
            pl.BlockSpec((rows, width), lambda p: (0, p)),
            pl.BlockSpec((1, width), lambda p: (0, p)),
        ),
    )


def mlp_grads_kernel(place, active, branch_grad, entry, hidden_grad, away_ref, kept_ref):
    half = active.shape[1] // 2
    for ref, core in ((away_ref, 1 - place[0]), (kept_ref, place[0])):
        column = rows_at(core * half, half, 128)
        ref[:half, :] = mm(active[:, column], branch_grad[...], TN)
        ref[half:, :] = mm(entry[:, column], hidden_grad[...], TN)


def mlp_grads(place, active, branch_grad, entry, hidden_grad):
    width = entry.shape[1]
    half = shape((width, width))
    operands = (place, active, branch_grad, entry, hidden_grad)
    return call(mlp_grads_kernel, "mlp_grads", (half, half), operands, smem=1)


def attn_grads_kernel(place, proj, entry, mixed, grad, away_ref, kept_ref, sums_ref, own_ref):
    columns = mixed.shape[0]
    for j in range(3):
        own_ref[j * columns : (j + 1) * columns, :] = proj[j, rows_at(place[2] * columns, columns, 16), :]
    sums_ref[...] = mm(jnp.ones((8, own_ref.shape[1]), LOW), own_ref[...], NT)
    inner, outer = 3 * columns // 2, columns // 2
    for ref, core in ((away_ref, 1 - place[0]), (kept_ref, place[0])):
        ref[:inner, :] = mm(own_ref[rows_at(core * inner, inner, 16), :], entry[...])
        ref[inner:, :] = mm(mixed[rows_at(core * outer, outer), :].astype(LOW), grad[...])


def attn_grads(place, proj, entry, mixed, grad):
    columns, tokens = mixed.shape
    width = entry.shape[1]
    half = shape((2 * columns, width))
    return call(
        attn_grads_kernel,
        "attn_grads",
        (half, half, shape((8, 3 * columns))),
        (place, proj, entry, mixed, grad),
        smem=1,
        scratch=[pltpu.VMEM((3 * columns, tokens), LOW)],
    )


def cut_kernel(shares, place, kept, other, *outs):
    for k, out in enumerate(outs):
        base, at = 0, 0
        for share in shares:
            row = rows_at(base + (place[1] ^ k) * share, share)
            out[at : at + share, :] = kept[row, :] + other[row, :]
            base, at = base + CHIPS * share, at + share


def place_kernel(shares, place, *refs):
    parts, out = refs[:-1], refs[-1]
    for k, part in enumerate(parts):
        base, at = 0, 0
        for share in shares:
            out[rows_at(base + (place[1] ^ k) * share, share), :] = part[at : at + share, :]
            base, at = base + CHIPS * share, at + share


def whole_kernel(shares, place, mine, other, *refs):
    outs, sems = refs[:-1], refs[-1]
    base, copies = 0, []
    for share, out in zip(shares, outs):
        half = CHIPS * share
        for part, core in ((mine, place[0]), (other, 1 - place[0])):
            target = out.at[rows_at(core * half, half), :]
            source = part.at[pl.ds(base, half), :]
            copies.append(pltpu.make_async_copy(source, target, sems.at[len(copies)]))
        base += half
    for copy in copies:
        copy.start()
    for copy in copies:
        copy.wait()


def flip(value, axis, count, mask):
    return lax.ppermute(value, axis, [(i, i ^ mask) for i in range(count)])


def cut_shares(place, away, kept, shares, n_dp):
    other = flip(away, "dp", n_dp, 1)
    part = shape((sum(shares), kept.shape[1]))
    return call(
        functools.partial(cut_kernel, shares), "cut", (part,) * CHIPS, (place, kept, other), smem=1
    )


def sum_shares(parts, n_dp, *others):
    moved = [flip(parts[k], "dp", n_dp, 2 * k) for k in range(1, CHIPS)]
    total = (tie(parts[0], *others) if others else parts[0]) + moved[0] + moved[1] + moved[2]
    masks = [1 << i for i in range(3, n_dp.bit_length() - 1)]
    return double(halve(total, n_dp, masks), n_dp, masks), moved


def spread_chips(share, n_dp):
    return [share] + [flip(share, "dp", n_dp, 2 * k) for k in range(1, CHIPS)]


def own_half(place, parts, shares):
    half = shape((CHIPS * sum(shares), parts[0].shape[1]))
    return call(functools.partial(place_kernel, shares), "place", half, (place, *parts), smem=1)


def both_halves(place, mine, other, shares):
    outs = tuple(shape((GROUP * count, mine.shape[1])) for count in shares)
    anywhere = pl.BlockSpec(memory_space=pl.ANY)
    return call(
        functools.partial(whole_kernel, shares),
        "whole",
        outs,
        (place, mine, other),
        smem=1,
        specs=[pl.BlockSpec(memory_space=pltpu.VMEM)] * 2,
        out_specs=(anywhere,) * len(outs),
        scratch=[pltpu.SemaphoreType.DMA((2 * len(outs),))],
    )


def halve(value, count, masks):
    index = lax.axis_index("dp")
    for mask in masks:
        half = value.shape[0] // 2
        side = (index // mask) % 2
        away = lax.dynamic_slice_in_dim(value, (1 - side) * half, half, 0)
        kept = lax.dynamic_slice_in_dim(value, side * half, half, 0)
        value = kept + flip(away, "dp", count, mask)
    return value


def double(value, count, masks):
    index = lax.axis_index("dp")
    for mask in reversed(masks):
        other = flip(value, "dp", count, mask)
        lower = (index // mask) % 2 == 0
        value = jnp.concatenate([jnp.where(lower, value, other), jnp.where(lower, other, value)])
    return value


def core_pair(rows, n_dp):
    other = flip(rows, "dp", n_dp, 1)
    first = lax.axis_index("dp") % 2 == 0
    return jnp.concatenate([jnp.where(first, rows, other), jnp.where(first, other, rows)])


def all_pairs(pair, n_dp):
    if n_dp != GROUP:
        pairs = lax.all_gather(pair, "dp").reshape(n_dp // 2, 2, *pair.shape)
        return pairs[:, 0].reshape(-1, pair.shape[1])
    chip = lax.axis_index("dp") // 2
    parts = [pair] + [flip(pair, "dp", n_dp, 2 * k) for k in range(1, CHIPS)]
    for bit in (1, 2):
        parts = [jnp.where(chip & bit != 0, parts[k ^ bit], parts[k]) for k in range(CHIPS)]
    return jnp.concatenate(parts)


def gather_rows(rows, n_dp):
    share = rows.shape[0] // n_dp
    mine = lax.dynamic_slice_in_dim(rows, lax.axis_index("dp") * share, share, 0)
    return lax.all_gather(mine.astype(FULL), ("tensor", "dp"), tiled=True)


def gather_z(rows, n_tensor):
    share = rows.shape[0] // GROUP
    start = (lax.axis_index("dp") % GROUP) * share
    mine = lax.dynamic_slice_in_dim(rows, start, share, 0).astype(FULL)
    return [mine] + [flip(mine, "tensor", n_tensor, k) for k in range(1, n_tensor)]


def gather_pieces(parts, n_dp):
    stacked = jnp.stack(parts)
    pieces = [stacked] + [flip(stacked, "dp", n_dp, 2 * k) for k in range(1, CHIPS)]
    return pieces + [flip(piece, "dp", n_dp, 1) for piece in pieces]


def tie_kernel(*refs):
    pass


def tie(value, *others):
    anywhere = pl.BlockSpec(memory_space=pl.ANY)
    return pl.pallas_call(
        tie_kernel,
        out_shape=jax.ShapeDtypeStruct(value.shape, value.dtype),
        in_specs=[anywhere] * (1 + len(others)),
        out_specs=anywhere,
        input_output_aliases={0: 0},
        name="tie",
    )(value, *others)


def as_one(function, *operands):
    shapes = jax.eval_shape(function, *operands)
    nothing = lambda *_: jax.tree.map(lambda leaf: jnp.zeros(leaf.shape, leaf.dtype), shapes)
    return lax.cond(lax.axis_index("dp") >= 0, function, nothing, *operands)


def per_device(
    n_dp,
    n_tensor,
    latents,
    condition,
    modulator,
    modulator_bias,
    attn_input,
    attn_input_bias,
    attn_output,
    attn_output_bias,
    ffn_input,
    ffn_input_bias,
    ffn_output,
    ffn_output_bias,
    cotangent,
):
    image_count, positions, features = latents.shape
    tokens = image_count * positions
    columns = attn_input.shape[2]
    z = lax.axis_index("tensor")
    member = lax.axis_index("dp") % GROUP
    place = jnp.stack([member % 2, member // 2, z]).astype(jnp.int32)
    inputs = latents.reshape(tokens, features)
    upstream = cotangent.reshape(tokens, features)
    weight_t = attn_input.swapaxes(1, 2)

    weight_wide = gather_rows(weight_t.reshape(-1, features), n_dp)
    weight_wide = weight_wide.reshape(n_tensor, 3, columns, features)
    cond_float = condition.astype(FULL)
    context_low = jax.nn.silu(cond_float).astype(LOW)

    def forward(context_low):
        def start(context_low):
            partial = mm(context_low, modulator)
            bias_own = jnp.stack(
                [attn_input_bias[0], jnp.zeros_like(attn_input_bias[0]), attn_input_bias[1]]
            )
            bias_row = jnp.zeros((3, n_tensor * columns), FULL)
            bias_row = lax.dynamic_update_slice_in_dim(bias_row, bias_own.astype(FULL), z * columns, 1)
            bias_row = bias_row.reshape(1, -1)
            bias_row = jnp.pad(bias_row, ((0, 0), (0, partial.shape[1] - bias_row.shape[1])))
            shared = jnp.concatenate([partial, bias_row])
            shared = [shared] + [flip(shared, "tensor", n_tensor, k) for k in range(1, n_tensor)]
            results = call(
                start_kernel,
                "start",
                (
                    shape((columns, tokens)),
                    shape((tokens, features), LOW),
                    shape((image_count, 6, features)),
                    shape((3, n_tensor * columns)),
                ),
                (*shared, modulator_bias[None], inputs, weight_t, bias_own),
            )
            return results, shared

        output_parts = gather_z(attn_output, n_tensor)
        (mixed_t, entry_one, modulation, bias_full), shared = start(context_low)
        output_parts = [tie(x, shared[-1]) for x in output_parts]
        near, far = (flip(mixed_t, "tensor", n_tensor, k) for k in (1, 2))
        inner = lax.ppermute(mixed_t, "tensor", [(1, 2), (2, 1)])
        outer = lax.ppermute(far, "tensor", [(1, 0), (2, 3)])
        mixed = [mixed_t, near, far, inner, outer]
        output_pieces = gather_pieces(output_parts, n_dp)
        attention, middle, entry_two, output_full = join_heads(
            place, mixed, output_pieces, attn_output_bias[None], inputs, modulation
        )
        hidden = mm(entry_two, ffn_input) + ffn_input_bias.astype(FULL)
        active, gelu_pull = jax.vjp(lambda inner: jax.nn.gelu(inner, approximate=True), hidden)
        active = active.astype(LOW)
        gate_two = modulation[:, None, 5]
        branch_grad = (gate_two * cotangent.astype(FULL)).astype(LOW).reshape(tokens, features)
        hidden_grad = gelu_pull(mm(branch_grad, ffn_output, NT))[0].astype(LOW)
        part = mm(hidden_grad, ffn_input, NT)
        first = mixed_t, entry_one, modulation, bias_full, attention, middle, output_full
        return first, (active, branch_grad, entry_two, hidden_grad), part

    first, mlp, part = as_one(forward, context_low)
    mixed_t, entry_one, modulation, bias_full, attention, middle, output_full = first
    entry_two_grad = lax.psum(part, "tensor")
    mlp_shares = (ffn_output.shape[0] // GROUP, features // GROUP)

    def beside_entry_two(place, mlp):
        active, branch_grad, entry_two, hidden_grad = mlp
        away, kept = mlp_grads(place, active, branch_grad, entry_two, hidden_grad)
        mlp_share = sum_shares(cut_shares(place, away, kept, mlp_shares, n_dp), n_dp)[0]
        branch_part = mm(active, ffn_output)
        weights = cotangent.astype(FULL)
        gate_part = jnp.sum(weights * branch_part.reshape(latents.shape), axis=1)
        parts = [gate_part] + [flip(gate_part, "tensor", n_tensor, k) for k in range(1, n_tensor)]
        gate_grad = (parts[0] + parts[1]) + (parts[2] + parts[3])
        gate_grad = gate_grad + ffn_output_bias.astype(FULL) * jnp.sum(weights, axis=1)
        sums = [jnp.sum(x.astype(FULL), axis=0) for x in (branch_grad, hidden_grad)]
        return mlp_share, branch_part, gate_grad, sums

    mlp_share, branch_part, gate_two_grad, mlp_sums = as_one(
        beside_entry_two, tie(place, part), mlp
    )

    def still_beside_entry_two(weight_wide, mlp_share):
        mlp_parts = spread_chips(mlp_share, n_dp)
        proj_full, weight_full = project_all(weight_wide, bias_full, entry_one)
        return mlp_parts, all_probs(proj_full, image_count), proj_full, weight_full

    mlp_parts, probs, proj_full, weight_full = as_one(
        still_beside_entry_two, tie(weight_wide, branch_part), mlp_share
    )
    entry_two_grad = tie(entry_two_grad, probs)
    entry_two_grad = tie(entry_two_grad, branch_part)
    branch_part = tie(branch_part, entry_two_grad)
    branch = lax.psum(branch_part, "tensor")
    attn_shares = (3 * columns // GROUP, columns // GROUP)

    def beside_branch(
        entry_two_grad, probs, proj_full, weight_full, gate_two_grad, mlp_sums, mlp_parts
    ):
        def heads(entry_two_grad, probs, proj_full):
            middle_grad, attention_grad, mixed_grad_t, middle_sums = middle_backward(
                entry_two_grad, middle, attention, upstream, modulation, output_full
            )
            proj_grad = attention_backward(probs, proj_full, mixed_grad_t)
            parts = attn_grads(place, proj_grad, entry_one, mixed_t, attention_grad)
            return middle_grad, middle_sums, proj_grad, parts

        middle_grad, middle_sums, proj_grad, (away, kept, own_sums) = as_one(
            heads, entry_two_grad, probs, proj_full
        )
        parts = cut_shares(place, away, kept, attn_shares, n_dp)

        def entry(proj_grad, weight_full, middle_grad):
            return entry_backward(
                proj_grad.reshape(-1, tokens),
                weight_full.reshape(-1, features),
                inputs,
                middle_grad,
                modulation,
            )

        latents_grad, entry_sums = as_one(
            entry, tie(proj_grad, parts[0]), weight_full, middle_grad
        )
        mlp_mine = own_half(place, [tie(mlp_parts[0], away), *mlp_parts[1:]], mlp_shares)
        mlp_other = flip(mlp_mine, "dp", n_dp, 1)
        modulation_grad = jnp.concatenate(
            [entry_sums, middle_sums[:, :3], gate_two_grad[:, None]], axis=1
        )
        modulation_grad = modulation_grad.reshape(image_count, -1).astype(LOW)
        attn_share, moved = sum_shares(parts, n_dp, entry_sums)
        sums = [mlp_sums[0], mlp_sums[1], jnp.sum(middle_sums[:, 3], axis=0), own_sums[0]]
        sizes = [x.shape[0] for x in sums]
        sums = jnp.pad(jnp.concatenate(sums)[None], ((0, image_count - 1), (0, 0)))
        context_wide = jnp.pad(context_low.astype(FULL), ((0, 0), (0, -context_low.shape[1] % 256)))
        small = [modulation_grad.astype(FULL), context_wide, sums]
        pair = core_pair(tie(jnp.concatenate(small, axis=1), *moved), n_dp)
        every = all_pairs(pair, n_dp)
        attn_parts = spread_chips(tie(attn_share, pair), n_dp)

        def finish(every, modulation_grad, mlp_mine, mlp_other):
            grad_modulator, grad_modulator_bias = modulator_backward(
                every, context_low.shape[1], context_wide.shape[1], features
            )
            sums = jnp.sum(every[:, 6 * features + context_wide.shape[1] :], axis=0)
            sums = jnp.split(sums, [sum(sizes[:i]) for i in (1, 2, 3)])
            context_grad = mm(modulation_grad, modulator, NT)
            condition_grad = jax.vjp(jax.nn.silu, cond_float)[1](context_grad)[0]
            mlp_whole = both_halves(place, mlp_mine, mlp_other, mlp_shares)
            return (grad_modulator, grad_modulator_bias), sums, condition_grad, mlp_whole

        modulator_grads, sums, condition_grad, mlp_whole = as_one(
            finish, every, modulation_grad, mlp_mine, mlp_other
        )
        attn_parts[0] = tie(attn_parts[0], condition_grad)
        attn_mine = own_half(place, attn_parts, attn_shares)
        attn_whole = both_halves(place, attn_mine, flip(attn_mine, "dp", n_dp, 1), attn_shares)
        return mlp_whole, attn_whole, latents_grad, condition_grad, modulator_grads, sums

    mlp_whole, attn_whole, latents_grad, condition_grad, modulator_grads, sums = as_one(
        beside_branch,
        tie(entry_two_grad, branch_part),
        probs,
        proj_full,
        weight_full,
        gate_two_grad,
        mlp_sums,
        mlp_parts,
    )
    grad_modulator, grad_modulator_bias = modulator_grads
    layer_out = end_forward(
        tie(branch, condition_grad), ffn_output_bias[None], middle, modulation
    )
    input_bias = sums[3].reshape(3, columns)
    return (
        layer_out.reshape(latents.shape),
        latents_grad.reshape(latents.shape),
        condition_grad,
        grad_modulator,
        grad_modulator_bias[0],
        attn_whole[0].reshape(3, columns, features).swapaxes(1, 2),
        jnp.stack([input_bias[0], input_bias[2]]),
        attn_whole[1],
        sums[2],
        mlp_whole[1],
        sums[1],
        mlp_whole[0],
        sums[0],
    )


def solution(mesh):
    placed = (
        P("dp", None, None),
        P("dp", "tensor"),
        P("tensor", None),
        P(),
        P(None, None, "tensor"),
        P(None, "tensor"),
        P("tensor", None),
        P(),
        P(None, "tensor"),
        P("tensor"),
        P("tensor", None),
        P(),
        P("dp", None, None),
    )
    return jax.shard_map(
        functools.partial(per_device, mesh.shape["dp"], mesh.shape["tensor"]),
        mesh=mesh,
        in_specs=placed,
        out_specs=(
            P("dp", None, None),
            P("dp", None, None),
            P("dp", "tensor"),
            P("tensor", None),
            P(),
            P(None, None, "tensor"),
            P(None, "tensor"),
            P("tensor", None),
            P(),
            P(None, "tensor"),
            P("tensor"),
            P("tensor", None),
            P(),
        ),
        check_vma=False,
    )
```

```python
import functools

import jax
import jax.numpy as jnp
from jax import lax
from jax.experimental import pallas as pl
from jax.experimental.pallas import tpu as pltpu
from jax.sharding import PartitionSpec as P

HEAD = 64
epsilon = 1e-06
SCALE = HEAD ** (-0.5)
LOW = jnp.bfloat16
FULL = jnp.float32
NN = (((1,), (0,)), ((), ()))
NT = (((1,), (1,)), ((), ()))
TN = (((0,), (0,)), ((), ()))
GROUP = 8
CHIPS = 4


def mm(left, right, dims=NN):
    return lax.dot_general(left, right, dims, preferred_element_type=FULL)


def norm_parts(values):
    centre = values - jnp.mean(values, axis=-1, keepdims=True)
    inverse = lax.rsqrt(jnp.mean(centre * centre, axis=-1, keepdims=True) + epsilon)
    return (centre * inverse, inverse)


def norm_back(grad, normed, inverse):
    return (
        grad
        - jnp.mean(grad, axis=-1, keepdims=True)
        - normed * jnp.mean(grad * normed, axis=-1, keepdims=True)
    ) * inverse


def shape(dims, dtype=FULL):
    return jax.ShapeDtypeStruct(dims, dtype)


def rows_at(start, count, step=8):
    return pl.ds(pl.multiple_of(start, step), count)


def call(kernel, name, out_shape, operands, smem=0, grid=None, specs=None, out_specs=None, scratch=()):
    vmem = pl.BlockSpec(memory_space=pltpu.VMEM)
    in_specs = [pl.BlockSpec(memory_space=pltpu.SMEM)] * smem
    in_specs += [vmem] * (len(operands) - smem) if specs is None else specs
    if out_specs is None:
        out_specs = jax.tree.map(lambda _: vmem, out_shape)
    extra = {} if grid is None else {"grid": grid}
    return pl.pallas_call(
        kernel,
        out_shape=out_shape,
        in_specs=in_specs,
        out_specs=out_specs,
        scratch_shapes=list(scratch),
        compiler_params=pltpu.CompilerParams(vmem_limit_bytes=48 * 2**20),
        name=name,
        **extra,
    )(*operands)


def bias_columns(row, count):
    return mm(row, jnp.ones((1, count), LOW), TN)


def softmax_t(keys_t, query_t):
    scores = mm(keys_t, query_t, TN) * SCALE
    shifted = jnp.exp(scores - jnp.max(scores, axis=0, keepdims=True))
    return shifted * (1.0 / jnp.sum(shifted, axis=0, keepdims=True))


def start_kernel(
    part0, part1, part2, part3, mod_bias, latents, weight, bias,
    mixed_ref, entry_ref, mod_ref,
):
    images, _, width = mod_ref.shape
    columns = weight.shape[1]
    positions = latents.shape[0] // images
    shared = (part0[...] + part1[...]) + (part2[...] + part3[...])
    modulation = shared + mod_bias[...].astype(FULL)
    for p in range(6):
        for g in range(images):
            mod_ref[g, p : p + 1, :] = modulation[g : g + 1, p * width : (p + 1) * width]
    offsets = [bias_columns(bias[j : j + 1, :], positions) for j in range(3)]
    for g in range(images):
        token = slice(g * positions, (g + 1) * positions)
        normed = norm_parts(latents[token, :].astype(FULL))[0]
        entry = (normed * (1.0 + mod_ref[g, 1:2, :]) + mod_ref[g, 0:1, :]).astype(LOW)
        entry_ref[token, :] = entry
        query, keys, values = (
            (mm(weight[j], entry, NT) + offsets[j]).astype(LOW) for j in range(3)
        )
        for h in range(columns // HEAD):
            row = slice(h * HEAD, (h + 1) * HEAD)
            probs = softmax_t(keys[row], query[row])
            mixed_ref[row, token] = mm(values[row], probs.astype(LOW)).astype(LOW).astype(FULL)


def probs_kernel(proj_ref, out_ref):
    for h in range(out_ref.shape[1]):
        row = slice(h * HEAD, (h + 1) * HEAD)
        out_ref[0, h] = softmax_t(proj_ref[1, row, :], proj_ref[0, row, :])


def all_probs(proj_t, images):
    _, width, tokens = proj_t.shape
    positions = tokens // images
    heads = width // HEAD
    step = 4 if heads % 4 == 0 else heads
    return call(
        probs_kernel,
        "all_probs",
        shape((images, heads, positions, positions)),
        (proj_t,),
        grid=(images, heads // step),
        specs=[pl.BlockSpec((2, step * HEAD, positions), lambda g, h: (0, h, g))],
        out_specs=pl.BlockSpec((1, step, positions, positions), lambda g, h: (g, h, 0, 0)),
    )


def backward_kernel(probs_ref, proj_ref, grad_ref, out_ref):
    for h in range(probs_ref.shape[1]):
        row = slice(h * HEAD, (h + 1) * HEAD)
        query, keys, values = proj_ref[0, row, :], proj_ref[1, row, :], proj_ref[2, row, :]
        grad = grad_ref[row, :]
        probs = probs_ref[0, h]
        probs_grad = mm(values, grad, TN)
        weighted = probs * probs_grad
        scores_grad = (weighted - probs * jnp.sum(weighted, axis=0, keepdims=True)).astype(LOW)
        out_ref[0, row, :] = (mm(keys, scores_grad) * SCALE).astype(LOW)
        out_ref[1, row, :] = (mm(query, scores_grad, NT) * SCALE).astype(LOW)
        out_ref[2, row, :] = mm(grad, probs.astype(LOW), NT).astype(LOW)


def attention_backward(probs, proj_t, grad_t):
    images, heads, positions, _ = probs.shape
    width, tokens = grad_t.shape
    step = 4 if heads % 4 == 0 else heads
    rows = step * HEAD
    block = pl.BlockSpec((3, rows, positions), lambda g, h: (0, h, g))
    return call(
        backward_kernel,
        "attention_backward",
        shape((3, width, tokens), LOW),
        (probs, proj_t, grad_t),
        grid=(images, heads // step),
        specs=[
            pl.BlockSpec((1, step, positions, positions), lambda g, h: (g, h, 0, 0)),
            block,
            pl.BlockSpec((rows, positions), lambda g, h: (h, g)),
        ],
        out_specs=block,
    )


def put_in_order(place, pieces, wide_ref):
    core, chip, z = place[0], place[1], place[2]
    groups, share, _ = pieces[0].shape
    rows = wide_ref.shape[0] // groups
    for m, piece in enumerate(pieces):
        owner = 2 * (chip ^ (m % CHIPS)) + (core ^ (m // CHIPS))
        for k in range(groups):
            start = (z ^ k) * rows + owner * share
            wide_ref[rows_at(start, share), :] = piece[k]


def join_kernel(place, mixed0, mixed1, mixed2, inner, outer, bias, inputs, mod, *refs):
    pieces, (attention_ref, middle_ref, entry_ref, low_ref, wide_ref, mixed_ref) = refs[:-6], refs[-6:]

    @pl.when(pl.program_id(0) == 0)
    def _():
        put_in_order(place, pieces, wide_ref)
        low_ref[...] = wide_ref[...].astype(LOW)

    mixed = (mixed0[...], mixed1[...], mixed2[...], inner[...] + outer[...])
    for k, part in enumerate(mixed):
        columns = part.shape[0]
        mixed_ref[rows_at((place[2] ^ k) * columns, columns, 16), :] = part.astype(LOW)
    attention = mm(mixed_ref[...], low_ref[...], TN) + bias[...].astype(FULL)
    attention_ref[...] = attention
    middle = inputs[...].astype(FULL) + mod[0, 2:3, :] * attention
    middle_ref[...] = middle
    normed = norm_parts(middle)[0]
    entry_ref[...] = (normed * (1.0 + mod[0, 4:5, :]) + mod[0, 3:4, :]).astype(LOW)


def join_heads(place, mixed, pieces, bias, inputs, modulation):
    images = modulation.shape[0]
    tokens, width = inputs.shape
    positions = tokens // images
    columns = mixed[0].shape[0]
    rows = columns * (len(mixed) - 1)
    by_image = pl.BlockSpec((positions, width), lambda g: (g, 0))
    specs = [pl.BlockSpec((columns, positions), lambda g: (0, g))] * len(mixed)
    specs += [pl.BlockSpec((1, width), lambda g: (0, 0)), by_image]
    specs += [pl.BlockSpec((1, 6, width), lambda g: (g, 0, 0))]
    specs += [pl.BlockSpec(pieces[0].shape, lambda g: (0, 0, 0))] * len(pieces)
    return call(
        join_kernel,
        "join_heads",
        (
            shape((tokens, width)),
            shape((tokens, width)),
            shape((tokens, width), LOW),
            shape((rows, width), LOW),
        ),
        (place, *mixed, bias, inputs, modulation, *pieces),
        smem=1,
        grid=(images,),
        specs=specs,
        out_specs=(by_image, by_image, by_image, pl.BlockSpec((rows, width), lambda g: (0, 0))),
        scratch=[pltpu.VMEM((rows, width), FULL), pltpu.VMEM((rows, positions), LOW)],
    )


def project_kernel(weight_ref, bias, entry, out_ref, low_ref):
    groups, _, columns, _ = weight_ref.shape
    for j in range(3):
        offsets = bias_columns(bias[j : j + 1, :].astype(LOW), entry.shape[0])
        for t in range(groups):
            weight = weight_ref[t, j].astype(LOW)
            row = slice(t * columns, (t + 1) * columns)
            low_ref[j, row, :] = weight
            out_ref[j, row, :] = (mm(weight, entry[...], NT) + offsets[row]).astype(LOW)


def project_all(weight, bias, entry):
    tokens, width = entry.shape
    rows = bias.shape[1]
    return call(
        project_kernel,
        "project_all",
        (shape((3, rows, tokens), LOW), shape((3, rows, width), LOW)),
        (weight, bias, entry),
    )


def middle_kernel(
    grad_ref, middle_ref, attention_ref, upstream_ref, mod_ref, weight_ref,
    middle_grad_ref, low_ref, mixed_grad_ref, sums_ref,
):
    grad = grad_ref[...]
    normed, inverse = norm_parts(middle_ref[...])
    sums_ref[0, 2:3, :] = jnp.sum(grad * normed, axis=0, keepdims=True)
    sums_ref[0, 1:2, :] = jnp.sum(grad, axis=0, keepdims=True)
    middle_grad = upstream_ref[...].astype(FULL)
    middle_grad = middle_grad + norm_back(grad * (1.0 + mod_ref[0, 4:5, :]), normed, inverse)
    middle_grad_ref[...] = middle_grad
    sums_ref[0, 0:1, :] = jnp.sum(middle_grad * attention_ref[...], axis=0, keepdims=True)
    low = (mod_ref[0, 2:3, :] * middle_grad).astype(LOW)
    low_ref[...] = low
    sums_ref[0, 3:4, :] = jnp.sum(low.astype(FULL), axis=0, keepdims=True)
    mixed_grad_ref[...] = mm(weight_ref[...], low, NT).astype(LOW)


def middle_backward(grad, middle, attention, upstream, modulation, weight):
    images = modulation.shape[0]
    tokens, width = grad.shape
    positions = tokens // images
    by_image = pl.BlockSpec((positions, width), lambda g: (g, 0))
    return call(
        middle_kernel,
        "middle_backward",
        (
            shape((tokens, width)),
            shape((tokens, width), LOW),
            shape((weight.shape[0], tokens), LOW),
            shape((images, 4, width)),
        ),
        (grad, middle, attention, upstream, modulation, weight),
        grid=(images,),
        specs=[by_image] * 4
        + [
            pl.BlockSpec((1, 6, width), lambda g: (g, 0, 0)),
            pl.BlockSpec(weight.shape, lambda g: (0, 0)),
        ],
        out_specs=(
            by_image,
            by_image,
            pl.BlockSpec((weight.shape[0], positions), lambda g: (0, g)),
            pl.BlockSpec((1, 4, width), lambda g: (g, 0, 0)),
        ),
    )


def entry_kernel(proj_ref, weight_ref, inputs_ref, middle_grad_ref, mod_ref, out_ref, sums_ref):
    grad = mm(proj_ref[...], weight_ref[...], TN)
    normed, inverse = norm_parts(inputs_ref[...].astype(FULL))
    sums_ref[0, 0:1, :] = jnp.sum(grad, axis=0, keepdims=True)
    sums_ref[0, 1:2, :] = jnp.sum(grad * normed, axis=0, keepdims=True)
    back = norm_back(grad * (1.0 + mod_ref[0, 1:2, :]), normed, inverse)
    out_ref[...] = middle_grad_ref[...] + back


def entry_backward(proj_grad, weight, inputs, middle_grad, modulation):
    images = modulation.shape[0]
    tokens, width = inputs.shape
    positions = tokens // images
    by_image = pl.BlockSpec((positions, width), lambda g: (g, 0))
    return call(
        entry_kernel,
        "entry_backward",
        (shape((tokens, width)), shape((images, 2, width))),
        (proj_grad, weight, inputs, middle_grad, modulation),
        grid=(images,),
        specs=[
            pl.BlockSpec((proj_grad.shape[0], positions), lambda g: (0, g)),
            pl.BlockSpec(weight.shape, lambda g: (0, 0)),
            by_image,
            by_image,
            pl.BlockSpec((1, 6, width), lambda g: (g, 0, 0)),
        ],
        out_specs=(by_image, pl.BlockSpec((1, 2, width), lambda g: (g, 0, 0))),
    )


def end_kernel(branch_ref, bias_ref, middle_ref, mod_ref, out_ref):
    branch = branch_ref[...] + bias_ref[...].astype(FULL)
    out_ref[...] = (middle_ref[...] + mod_ref[0, 5:6, :] * branch).astype(LOW)


def end_forward(branch, bias, middle, modulation):
    images = modulation.shape[0]
    tokens, width = middle.shape
    by_image = pl.BlockSpec((tokens // images, width), lambda g: (g, 0))
    return call(
        end_kernel,
        "end_forward",
        shape((tokens, width), LOW),
        (branch, bias, middle, modulation),
        grid=(images,),
        specs=[
            by_image,
            pl.BlockSpec((1, width), lambda g: (0, 0)),
            by_image,
            pl.BlockSpec((1, 6, width), lambda g: (g, 0, 0)),
        ],
        out_specs=by_image,
    )


def modulator_kernel(every_ref, context_ref, out_ref, sums_ref):
    part = every_ref[...]
    sums_ref[...] = jnp.sum(part, axis=0, keepdims=True)
    context = context_ref[:, : out_ref.shape[0]].astype(LOW)
    out_ref[...] = mm(context, part.astype(LOW), TN)


def modulator_backward(every, rows, context_width, width):
    images = every.shape[0]
    at = 6 * width // context_width
    return call(
        modulator_kernel,
        "modulator_backward",
        (shape((rows, 6 * width)), shape((1, 6 * width))),
        (every, every),
        grid=(6,),
        specs=[
            pl.BlockSpec((images, width), lambda p: (0, p)),
            pl.BlockSpec((images, context_width), lambda p: (0, at)),
        ],
        out_specs=(
            pl.BlockSpec((rows, width), lambda p: (0, p)),
            pl.BlockSpec((1, width), lambda p: (0, p)),
        ),
    )


def mlp_grads_kernel(place, active, branch_grad, entry, hidden_grad, away_ref, kept_ref):
    half = active.shape[1] // 2
    for ref, core in ((away_ref, 1 - place[0]), (kept_ref, place[0])):
        column = rows_at(core * half, half, 128)
        ref[:half, :] = mm(active[:, column], branch_grad[...], TN)
        ref[half:, :] = mm(entry[:, column], hidden_grad[...], TN)


def mlp_grads(place, active, branch_grad, entry, hidden_grad):
    width = entry.shape[1]
    half = shape((width, width))
    operands = (place, active, branch_grad, entry, hidden_grad)
    return call(mlp_grads_kernel, "mlp_grads", (half, half), operands, smem=1)


def attn_grads_kernel(place, proj, entry, mixed, grad, away_ref, kept_ref, sums_ref, own_ref):
    columns = mixed.shape[0]
    for j in range(3):
        own_ref[j * columns : (j + 1) * columns, :] = proj[j, rows_at(place[2] * columns, columns, 16), :]
    sums_ref[...] = mm(jnp.ones((8, own_ref.shape[1]), LOW), own_ref[...], NT)
    inner, outer = 3 * columns // 2, columns // 2
    for ref, core in ((away_ref, 1 - place[0]), (kept_ref, place[0])):
        ref[:inner, :] = mm(own_ref[rows_at(core * inner, inner, 16), :], entry[...])
        ref[inner:, :] = mm(mixed[rows_at(core * outer, outer), :].astype(LOW), grad[...])


def attn_grads(place, proj, entry, mixed, grad):
    columns, tokens = mixed.shape
    width = entry.shape[1]
    half = shape((2 * columns, width))
    return call(
        attn_grads_kernel,
        "attn_grads",
        (half, half, shape((8, 3 * columns))),
        (place, proj, entry, mixed, grad),
        smem=1,
        scratch=[pltpu.VMEM((3 * columns, tokens), LOW)],
    )


def cut_kernel(shares, place, kept, other, *outs):
    for k, out in enumerate(outs):
        base, at = 0, 0
        for share in shares:
            row = rows_at(base + (place[1] ^ k) * share, share)
            out[at : at + share, :] = kept[row, :] + other[row, :]
            base, at = base + CHIPS * share, at + share


def place_kernel(shares, place, *refs):
    parts, out = refs[:-1], refs[-1]
    for k, part in enumerate(parts):
        base, at = 0, 0
        for share in shares:
            out[rows_at(base + (place[1] ^ k) * share, share), :] = part[at : at + share, :]
            base, at = base + CHIPS * share, at + share


def whole_kernel(shares, place, mine, other, *refs):
    outs, sems = refs[:-1], refs[-1]
    base, copies = 0, []
    for share, out in zip(shares, outs):
        half = CHIPS * share
        for part, core in ((mine, place[0]), (other, 1 - place[0])):
            target = out.at[rows_at(core * half, half), :]
            source = part.at[pl.ds(base, half), :]
            copies.append(pltpu.make_async_copy(source, target, sems.at[len(copies)]))
        base += half
    for copy in copies:
        copy.start()
    for copy in copies:
        copy.wait()


def flip(value, axis, count, mask):
    return lax.ppermute(value, axis, [(i, i ^ mask) for i in range(count)])


def cut_shares(place, away, kept, shares, n_dp):
    other = flip(away, "dp", n_dp, 1)
    part = shape((sum(shares), kept.shape[1]))
    return call(
        functools.partial(cut_kernel, shares), "cut", (part,) * CHIPS, (place, kept, other), smem=1
    )


def sum_shares(parts, n_dp, *others):
    moved = [flip(parts[k], "dp", n_dp, 2 * k) for k in range(1, CHIPS)]
    total = (tie(parts[0], *others) if others else parts[0]) + moved[0] + moved[1] + moved[2]
    masks = [1 << i for i in range(3, n_dp.bit_length() - 1)]
    return double(halve(total, n_dp, masks), n_dp, masks), moved


def spread_chips(share, n_dp):
    return [share] + [flip(share, "dp", n_dp, 2 * k) for k in range(1, CHIPS)]


def own_half(place, parts, shares):
    half = shape((CHIPS * sum(shares), parts[0].shape[1]))
    return call(functools.partial(place_kernel, shares), "place", half, (place, *parts), smem=1)


def both_halves(place, mine, other, shares):
    outs = tuple(shape((GROUP * count, mine.shape[1])) for count in shares)
    anywhere = pl.BlockSpec(memory_space=pl.ANY)
    return call(
        functools.partial(whole_kernel, shares),
        "whole",
        outs,
        (place, mine, other),
        smem=1,
        specs=[pl.BlockSpec(memory_space=pltpu.VMEM)] * 2,
        out_specs=(anywhere,) * len(outs),
        scratch=[pltpu.SemaphoreType.DMA((2 * len(outs),))],
    )


def halve(value, count, masks):
    index = lax.axis_index("dp")
    for mask in masks:
        half = value.shape[0] // 2
        side = (index // mask) % 2
        away = lax.dynamic_slice_in_dim(value, (1 - side) * half, half, 0)
        kept = lax.dynamic_slice_in_dim(value, side * half, half, 0)
        value = kept + flip(away, "dp", count, mask)
    return value


def double(value, count, masks):
    index = lax.axis_index("dp")
    for mask in reversed(masks):
        other = flip(value, "dp", count, mask)
        lower = (index // mask) % 2 == 0
        value = jnp.concatenate([jnp.where(lower, value, other), jnp.where(lower, other, value)])
    return value


def core_pair(rows, n_dp):
    other = flip(rows, "dp", n_dp, 1)
    first = lax.axis_index("dp") % 2 == 0
    return jnp.concatenate([jnp.where(first, rows, other), jnp.where(first, other, rows)])


def all_pairs(pair, n_dp):
    if n_dp != GROUP:
        pairs = lax.all_gather(pair, "dp").reshape(n_dp // 2, 2, *pair.shape)
        return pairs[:, 0].reshape(-1, pair.shape[1])
    chip = lax.axis_index("dp") // 2
    parts = [pair] + [flip(pair, "dp", n_dp, 2 * k) for k in range(1, CHIPS)]
    for bit in (1, 2):
        parts = [jnp.where(chip & bit != 0, parts[k ^ bit], parts[k]) for k in range(CHIPS)]
    return jnp.concatenate(parts)


def gather_rows(rows, n_dp):
    share = rows.shape[0] // n_dp
    mine = lax.dynamic_slice_in_dim(rows, lax.axis_index("dp") * share, share, 0)
    return lax.all_gather(mine.astype(FULL), ("tensor", "dp"), tiled=True)


def gather_z(rows, n_tensor):
    share = rows.shape[0] // GROUP
    start = (lax.axis_index("dp") % GROUP) * share
    mine = lax.dynamic_slice_in_dim(rows, start, share, 0).astype(FULL)
    return [mine] + [flip(mine, "tensor", n_tensor, k) for k in range(1, n_tensor)]


def gather_pieces(parts, n_dp):
    stacked = jnp.stack(parts)
    pieces = [stacked] + [flip(stacked, "dp", n_dp, 2 * k) for k in range(1, CHIPS)]
    return pieces + [flip(piece, "dp", n_dp, 1) for piece in pieces]


def tie_kernel(*refs):
    pass


def tie(value, *others):
    anywhere = pl.BlockSpec(memory_space=pl.ANY)
    return pl.pallas_call(
        tie_kernel,
        out_shape=jax.ShapeDtypeStruct(value.shape, value.dtype),
        in_specs=[anywhere] * (1 + len(others)),
        out_specs=anywhere,
        input_output_aliases={0: 0},
        name="tie",
    )(value, *others)


def as_one(function, *operands):
    shapes = jax.eval_shape(function, *operands)
    nothing = lambda *_: jax.tree.map(lambda leaf: jnp.zeros(leaf.shape, leaf.dtype), shapes)
    return lax.cond(lax.axis_index("dp") >= 0, function, nothing, *operands)


def per_device(
    n_dp,
    n_tensor,
    latents,
    condition,
    modulator,
    modulator_bias,
    attn_input,
    attn_input_bias,
    attn_output,
    attn_output_bias,
    ffn_input,
    ffn_input_bias,
    ffn_output,
    ffn_output_bias,
    cotangent,
):
    image_count, positions, features = latents.shape
    tokens = image_count * positions
    columns = attn_input.shape[2]
    z = lax.axis_index("tensor")
    member = lax.axis_index("dp") % GROUP
    place = jnp.stack([member % 2, member // 2, z]).astype(jnp.int32)
    inputs = latents.reshape(tokens, features)
    upstream = cotangent.reshape(tokens, features)
    weight_t = attn_input.swapaxes(1, 2)

    weight_wide = gather_rows(weight_t.reshape(-1, features), n_dp)
    weight_wide = weight_wide.reshape(n_tensor, 3, columns, features)
    cond_float = condition.astype(FULL)
    context_low = jax.nn.silu(cond_float).astype(LOW)

    bias_own = jnp.stack(
        [attn_input_bias[0], jnp.zeros_like(attn_input_bias[0]), attn_input_bias[1]]
    )

    def forward(context_low):
        def start(context_low):
            shared = mm(context_low, modulator)
            shared = [shared] + [flip(shared, "tensor", n_tensor, k) for k in range(1, n_tensor)]
            results = call(
                start_kernel,
                "start",
                (
                    shape((columns, tokens)),
                    shape((tokens, features), LOW),
                    shape((image_count, 6, features)),
                ),
                (*shared, modulator_bias[None], inputs, weight_t, bias_own),
            )
            return results, shared

        output_parts = gather_z(attn_output, n_tensor)
        (mixed_t, entry_one, modulation), shared = start(context_low)
        output_parts = [tie(x, shared[-1]) for x in output_parts]
        near, far = (flip(mixed_t, "tensor", n_tensor, k) for k in (1, 2))
        inner = lax.ppermute(mixed_t, "tensor", [(1, 2), (2, 1)])
        outer = lax.ppermute(far, "tensor", [(1, 0), (2, 3)])
        mixed = [mixed_t, near, far, inner, outer]
        output_pieces = gather_pieces(output_parts, n_dp)
        attention, middle, entry_two, output_full = join_heads(
            place, mixed, output_pieces, attn_output_bias[None], inputs, modulation
        )
        hidden = mm(entry_two, ffn_input) + ffn_input_bias.astype(FULL)
        active, gelu_pull = jax.vjp(lambda inner: jax.nn.gelu(inner, approximate=True), hidden)
        active = active.astype(LOW)
        gate_two = modulation[:, None, 5]
        branch_grad = (gate_two * cotangent.astype(FULL)).astype(LOW).reshape(tokens, features)
        hidden_grad = gelu_pull(mm(branch_grad, ffn_output, NT))[0].astype(LOW)
        part = mm(hidden_grad, ffn_input, NT)
        first = mixed_t, entry_one, modulation, attention, middle, output_full
        return first, (active, branch_grad, entry_two, hidden_grad), part

    first, mlp, part = as_one(forward, context_low)
    mixed_t, entry_one, modulation, attention, middle, output_full = first
    entry_two_grad = lax.psum(part, "tensor")
    mlp_shares = (ffn_output.shape[0] // GROUP, features // GROUP)

    def beside_entry_two(place, mlp):
        active, branch_grad, entry_two, hidden_grad = mlp
        away, kept = mlp_grads(place, active, branch_grad, entry_two, hidden_grad)
        mlp_share = sum_shares(cut_shares(place, away, kept, mlp_shares, n_dp), n_dp)[0]
        branch_part = mm(active, ffn_output)
        weights = cotangent.astype(FULL)
        gate_part = jnp.sum(weights * branch_part.reshape(latents.shape), axis=1)
        bias_row = jnp.zeros((3, n_tensor * columns), FULL)
        bias_row = lax.dynamic_update_slice_in_dim(bias_row, bias_own.astype(FULL), z * columns, 1)
        part = jnp.concatenate([gate_part, bias_row])
        parts = [part] + [flip(part, "tensor", n_tensor, k) for k in range(1, n_tensor)]
        part = (parts[0] + parts[1]) + (parts[2] + parts[3])
        gate_grad = part[:image_count] + ffn_output_bias.astype(FULL) * jnp.sum(weights, axis=1)
        sums = [jnp.sum(x.astype(FULL), axis=0) for x in (branch_grad, hidden_grad)]
        return mlp_share, branch_part, gate_grad, part[image_count:], sums

    mlp_share, branch_part, gate_two_grad, bias_full, mlp_sums = as_one(
        beside_entry_two, tie(place, part), mlp
    )

    def still_beside_entry_two(weight_wide, mlp_share):
        mlp_parts = spread_chips(mlp_share, n_dp)
        proj_full, weight_full = project_all(weight_wide, bias_full, entry_one)
        return mlp_parts, all_probs(proj_full, image_count), proj_full, weight_full

    mlp_parts, probs, proj_full, weight_full = as_one(
        still_beside_entry_two, tie(weight_wide, branch_part), mlp_share
    )
    entry_two_grad = tie(entry_two_grad, probs)
    entry_two_grad = tie(entry_two_grad, branch_part)
    branch_part = tie(branch_part, entry_two_grad)
    branch = lax.psum(branch_part, "tensor")
    attn_shares = (3 * columns // GROUP, columns // GROUP)

    def beside_branch(
        entry_two_grad, probs, proj_full, weight_full, gate_two_grad, mlp_sums, mlp_parts
    ):
        def heads(entry_two_grad, probs, proj_full):
            middle_grad, attention_grad, mixed_grad_t, middle_sums = middle_backward(
                entry_two_grad, middle, attention, upstream, modulation, output_full
            )
            proj_grad = attention_backward(probs, proj_full, mixed_grad_t)
            parts = attn_grads(place, proj_grad, entry_one, mixed_t, attention_grad)
            return middle_grad, middle_sums, proj_grad, parts

        middle_grad, middle_sums, proj_grad, (away, kept, own_sums) = as_one(
            heads, entry_two_grad, probs, proj_full
        )
        parts = cut_shares(place, away, kept, attn_shares, n_dp)

        def entry(proj_grad, weight_full, middle_grad):
            return entry_backward(
                proj_grad.reshape(-1, tokens),
                weight_full.reshape(-1, features),
                inputs,
                middle_grad,
                modulation,
            )

        latents_grad, entry_sums = as_one(
            entry, tie(proj_grad, parts[0]), weight_full, middle_grad
        )
        mlp_mine = own_half(place, [tie(mlp_parts[0], away), *mlp_parts[1:]], mlp_shares)
        mlp_other = flip(mlp_mine, "dp", n_dp, 1)
        modulation_grad = jnp.concatenate(
            [entry_sums, middle_sums[:, :3], gate_two_grad[:, None]], axis=1
        )
        modulation_grad = modulation_grad.reshape(image_count, -1).astype(LOW)
        attn_share, moved = sum_shares(parts, n_dp, entry_sums)
        sums = [mlp_sums[0], mlp_sums[1], jnp.sum(middle_sums[:, 3], axis=0), own_sums[0]]
        sizes = [x.shape[0] for x in sums]
        sums = jnp.pad(jnp.concatenate(sums)[None], ((0, image_count - 1), (0, 0)))
        context_wide = jnp.pad(context_low.astype(FULL), ((0, 0), (0, -context_low.shape[1] % 256)))
        small = [modulation_grad.astype(FULL), context_wide, sums]
        pair = core_pair(tie(jnp.concatenate(small, axis=1), *moved), n_dp)
        every = all_pairs(pair, n_dp)
        attn_parts = spread_chips(tie(attn_share, pair), n_dp)

        def finish(every, modulation_grad, mlp_mine, mlp_other):
            grad_modulator, grad_modulator_bias = modulator_backward(
                every, context_low.shape[1], context_wide.shape[1], features
            )
            sums = jnp.sum(every[:, 6 * features + context_wide.shape[1] :], axis=0)
            sums = jnp.split(sums, [sum(sizes[:i]) for i in (1, 2, 3)])
            context_grad = mm(modulation_grad, modulator, NT)
            condition_grad = jax.vjp(jax.nn.silu, cond_float)[1](context_grad)[0]
            mlp_whole = both_halves(place, mlp_mine, mlp_other, mlp_shares)
            return (grad_modulator, grad_modulator_bias), sums, condition_grad, mlp_whole

        modulator_grads, sums, condition_grad, mlp_whole = as_one(
            finish, every, modulation_grad, mlp_mine, mlp_other
        )
        attn_parts[0] = tie(attn_parts[0], condition_grad)
        attn_mine = own_half(place, attn_parts, attn_shares)
        attn_whole = both_halves(place, attn_mine, flip(attn_mine, "dp", n_dp, 1), attn_shares)
        return mlp_whole, attn_whole, latents_grad, condition_grad, modulator_grads, sums

    mlp_whole, attn_whole, latents_grad, condition_grad, modulator_grads, sums = as_one(
        beside_branch,
        tie(entry_two_grad, branch_part),
        probs,
        proj_full,
        weight_full,
        gate_two_grad,
        mlp_sums,
        mlp_parts,
    )
    grad_modulator, grad_modulator_bias = modulator_grads
    layer_out = end_forward(
        tie(branch, condition_grad), ffn_output_bias[None], middle, modulation
    )
    input_bias = sums[3].reshape(3, columns)
    return (
        layer_out.reshape(latents.shape),
        latents_grad.reshape(latents.shape),
        condition_grad,
        grad_modulator,
        grad_modulator_bias[0],
        attn_whole[0].reshape(3, columns, features).swapaxes(1, 2),
        jnp.stack([input_bias[0], input_bias[2]]),
        attn_whole[1],
        sums[2],
        mlp_whole[1],
        sums[1],
        mlp_whole[0],
        sums[0],
    )


def solution(mesh):
    placed = (
        P("dp", None, None),
        P("dp", "tensor"),
        P("tensor", None),
        P(),
        P(None, None, "tensor"),
        P(None, "tensor"),
        P("tensor", None),
        P(),
        P(None, "tensor"),
        P("tensor"),
        P("tensor", None),
        P(),
        P("dp", None, None),
    )
    return jax.shard_map(
        functools.partial(per_device, mesh.shape["dp"], mesh.shape["tensor"]),
        mesh=mesh,
        in_specs=placed,
        out_specs=(
            P("dp", None, None),
            P("dp", None, None),
            P("dp", "tensor"),
            P("tensor", None),
            P(),
            P(None, None, "tensor"),
            P(None, "tensor"),
            P("tensor", None),
            P(),
            P(None, "tensor"),
            P("tensor"),
            P("tensor", None),
            P(),
        ),
        check_vma=False,
    )
```

```python
import functools

import jax
import jax.numpy as jnp
from jax import lax
from jax.experimental import pallas as pl
from jax.experimental.pallas import tpu as pltpu
from jax.sharding import PartitionSpec as P

HEAD = 64
epsilon = 1e-06
SCALE = HEAD ** (-0.5)
LOW = jnp.bfloat16
FULL = jnp.float32
NN = (((1,), (0,)), ((), ()))
NT = (((1,), (1,)), ((), ()))
TN = (((0,), (0,)), ((), ()))
GROUP = 8
CHIPS = 4


def mm(left, right, dims=NN):
    return lax.dot_general(left, right, dims, preferred_element_type=FULL)


def norm_parts(values):
    centre = values - jnp.mean(values, axis=-1, keepdims=True)
    inverse = lax.rsqrt(jnp.mean(centre * centre, axis=-1, keepdims=True) + epsilon)
    return (centre * inverse, inverse)


def norm_back(grad, normed, inverse):
    return (
        grad
        - jnp.mean(grad, axis=-1, keepdims=True)
        - normed * jnp.mean(grad * normed, axis=-1, keepdims=True)
    ) * inverse


def shape(dims, dtype=FULL):
    return jax.ShapeDtypeStruct(dims, dtype)


def rows_at(start, count, step=8):
    return pl.ds(pl.multiple_of(start, step), count)


def call(kernel, name, out_shape, operands, smem=0, grid=None, specs=None, out_specs=None, scratch=()):
    vmem = pl.BlockSpec(memory_space=pltpu.VMEM)
    in_specs = [pl.BlockSpec(memory_space=pltpu.SMEM)] * smem
    in_specs += [vmem] * (len(operands) - smem) if specs is None else specs
    if out_specs is None:
        out_specs = jax.tree.map(lambda _: vmem, out_shape)
    extra = {} if grid is None else {"grid": grid}
    return pl.pallas_call(
        kernel,
        out_shape=out_shape,
        in_specs=in_specs,
        out_specs=out_specs,
        scratch_shapes=list(scratch),
        compiler_params=pltpu.CompilerParams(vmem_limit_bytes=48 * 2**20),
        name=name,
        **extra,
    )(*operands)


def bias_columns(row, count):
    return mm(row, jnp.ones((1, count), LOW), TN)


def softmax_t(keys_t, query_t):
    scores = mm(keys_t, query_t, TN) * SCALE
    shifted = jnp.exp(scores - jnp.max(scores, axis=0, keepdims=True))
    return shifted * (1.0 / jnp.sum(shifted, axis=0, keepdims=True))


def start_kernel(
    part0, part1, part2, part3, mod_bias, latents, weight, bias,
    mixed_ref, entry_ref, mod_ref,
):
    images, _, width = mod_ref.shape
    columns = weight.shape[1]
    positions = latents.shape[0] // images
    shared = (part0[...] + part1[...]) + (part2[...] + part3[...])
    modulation = shared + mod_bias[...].astype(FULL)
    for p in range(6):
        for g in range(images):
            mod_ref[g, p : p + 1, :] = modulation[g : g + 1, p * width : (p + 1) * width]
    offsets = [bias_columns(bias[j : j + 1, :], positions) for j in range(3)]
    for g in range(images):
        token = slice(g * positions, (g + 1) * positions)
        normed = norm_parts(latents[token, :].astype(FULL))[0]
        entry = (normed * (1.0 + mod_ref[g, 1:2, :]) + mod_ref[g, 0:1, :]).astype(LOW)
        entry_ref[token, :] = entry
        query, keys, values = (
            (mm(weight[j], entry, NT) + offsets[j]).astype(LOW) for j in range(3)
        )
        for h in range(columns // HEAD):
            row = slice(h * HEAD, (h + 1) * HEAD)
            probs = softmax_t(keys[row], query[row])
            mixed_ref[row, token] = mm(values[row], probs.astype(LOW)).astype(LOW).astype(FULL)


def probs_kernel(proj_ref, out_ref):
    for h in range(out_ref.shape[1]):
        row = slice(h * HEAD, (h + 1) * HEAD)
        out_ref[0, h] = softmax_t(proj_ref[1, row, :], proj_ref[0, row, :])


def all_probs(proj_t, images):
    _, width, tokens = proj_t.shape
    positions = tokens // images
    heads = width // HEAD
    step = 4 if heads % 4 == 0 else heads
    return call(
        probs_kernel,
        "all_probs",
        shape((images, heads, positions, positions)),
        (proj_t,),
        grid=(images, heads // step),
        specs=[pl.BlockSpec((2, step * HEAD, positions), lambda g, h: (0, h, g))],
        out_specs=pl.BlockSpec((1, step, positions, positions), lambda g, h: (g, h, 0, 0)),
    )


def backward_kernel(probs_ref, proj_ref, grad_ref, out_ref):
    for h in range(probs_ref.shape[1]):
        row = slice(h * HEAD, (h + 1) * HEAD)
        query, keys, values = proj_ref[0, row, :], proj_ref[1, row, :], proj_ref[2, row, :]
        grad = grad_ref[row, :]
        probs = probs_ref[0, h]
        probs_grad = mm(values, grad, TN)
        weighted = probs * probs_grad
        scores_grad = (weighted - probs * jnp.sum(weighted, axis=0, keepdims=True)).astype(LOW)
        out_ref[0, row, :] = (mm(keys, scores_grad) * SCALE).astype(LOW)
        out_ref[1, row, :] = (mm(query, scores_grad, NT) * SCALE).astype(LOW)
        out_ref[2, row, :] = mm(grad, probs.astype(LOW), NT).astype(LOW)


def attention_backward(probs, proj_t, grad_t):
    images, heads, positions, _ = probs.shape
    width, tokens = grad_t.shape
    step = 4 if heads % 4 == 0 else heads
    rows = step * HEAD
    block = pl.BlockSpec((3, rows, positions), lambda g, h: (0, h, g))
    return call(
        backward_kernel,
        "attention_backward",
        shape((3, width, tokens), LOW),
        (probs, proj_t, grad_t),
        grid=(images, heads // step),
        specs=[
            pl.BlockSpec((1, step, positions, positions), lambda g, h: (g, h, 0, 0)),
            block,
            pl.BlockSpec((rows, positions), lambda g, h: (h, g)),
        ],
        out_specs=block,
    )


def put_in_order(place, pieces, wide_ref):
    core, chip, z = place[0], place[1], place[2]
    groups, share, _ = pieces[0].shape
    rows = wide_ref.shape[0] // groups
    for m, piece in enumerate(pieces):
        owner = 2 * (chip ^ (m % CHIPS)) + (core ^ (m // CHIPS))
        for k in range(groups):
            start = (z ^ k) * rows + owner * share
            wide_ref[rows_at(start, share), :] = piece[k]


def join_kernel(place, mixed0, mixed1, mixed2, inner, outer, bias, inputs, mod, *refs):
    pieces, (attention_ref, middle_ref, entry_ref, low_ref, wide_ref, mixed_ref) = refs[:-6], refs[-6:]

    @pl.when(pl.program_id(0) == 0)
    def _():
        put_in_order(place, pieces, wide_ref)
        low_ref[...] = wide_ref[...].astype(LOW)

    mixed = (mixed0[...], mixed1[...], mixed2[...], inner[...] + outer[...])
    for k, part in enumerate(mixed):
        columns = part.shape[0]
        mixed_ref[rows_at((place[2] ^ k) * columns, columns, 16), :] = part.astype(LOW)
    attention = mm(mixed_ref[...], low_ref[...], TN) + bias[...].astype(FULL)
    attention_ref[...] = attention
    middle = inputs[...].astype(FULL) + mod[0, 2:3, :] * attention
    middle_ref[...] = middle
    normed = norm_parts(middle)[0]
    entry_ref[...] = (normed * (1.0 + mod[0, 4:5, :]) + mod[0, 3:4, :]).astype(LOW)


def join_heads(place, mixed, pieces, bias, inputs, modulation):
    images = modulation.shape[0]
    tokens, width = inputs.shape
    positions = tokens // images
    columns = mixed[0].shape[0]
    rows = columns * (len(mixed) - 1)
    by_image = pl.BlockSpec((positions, width), lambda g: (g, 0))
    specs = [pl.BlockSpec((columns, positions), lambda g: (0, g))] * len(mixed)
    specs += [pl.BlockSpec((1, width), lambda g: (0, 0)), by_image]
    specs += [pl.BlockSpec((1, 6, width), lambda g: (g, 0, 0))]
    specs += [pl.BlockSpec(pieces[0].shape, lambda g: (0, 0, 0))] * len(pieces)
    return call(
        join_kernel,
        "join_heads",
        (
            shape((tokens, width)),
            shape((tokens, width)),
            shape((tokens, width), LOW),
            shape((rows, width), LOW),
        ),
        (place, *mixed, bias, inputs, modulation, *pieces),
        smem=1,
        grid=(images,),
        specs=specs,
        out_specs=(by_image, by_image, by_image, pl.BlockSpec((rows, width), lambda g: (0, 0))),
        scratch=[pltpu.VMEM((rows, width), FULL), pltpu.VMEM((rows, positions), LOW)],
    )


def project_kernel(weight_ref, bias, entry, out_ref, low_ref):
    groups, _, columns, _ = weight_ref.shape
    for j in range(3):
        offsets = bias_columns(bias[j : j + 1, :].astype(LOW), entry.shape[0])
        for t in range(groups):
            weight = weight_ref[t, j].astype(LOW)
            row = slice(t * columns, (t + 1) * columns)
            low_ref[j, row, :] = weight
            out_ref[j, row, :] = (mm(weight, entry[...], NT) + offsets[row]).astype(LOW)


def project_all(weight, bias, entry):
    tokens, width = entry.shape
    rows = bias.shape[1]
    return call(
        project_kernel,
        "project_all",
        (shape((3, rows, tokens), LOW), shape((3, rows, width), LOW)),
        (weight, bias, entry),
    )


def middle_kernel(
    grad_ref, middle_ref, attention_ref, upstream_ref, mod_ref, weight_ref,
    middle_grad_ref, low_ref, mixed_grad_ref, sums_ref,
):
    grad = grad_ref[...]
    normed, inverse = norm_parts(middle_ref[...])
    sums_ref[0, 2:3, :] = jnp.sum(grad * normed, axis=0, keepdims=True)
    sums_ref[0, 1:2, :] = jnp.sum(grad, axis=0, keepdims=True)
    middle_grad = upstream_ref[...].astype(FULL)
    middle_grad = middle_grad + norm_back(grad * (1.0 + mod_ref[0, 4:5, :]), normed, inverse)
    middle_grad_ref[...] = middle_grad
    sums_ref[0, 0:1, :] = jnp.sum(middle_grad * attention_ref[...], axis=0, keepdims=True)
    low = (mod_ref[0, 2:3, :] * middle_grad).astype(LOW)
    low_ref[...] = low
    sums_ref[0, 3:4, :] = jnp.sum(low.astype(FULL), axis=0, keepdims=True)
    mixed_grad_ref[...] = mm(weight_ref[...], low, NT).astype(LOW)


def middle_backward(grad, middle, attention, upstream, modulation, weight):
    images = modulation.shape[0]
    tokens, width = grad.shape
    positions = tokens // images
    by_image = pl.BlockSpec((positions, width), lambda g: (g, 0))
    return call(
        middle_kernel,
        "middle_backward",
        (
            shape((tokens, width)),
            shape((tokens, width), LOW),
            shape((weight.shape[0], tokens), LOW),
            shape((images, 4, width)),
        ),
        (grad, middle, attention, upstream, modulation, weight),
        grid=(images,),
        specs=[by_image] * 4
        + [
            pl.BlockSpec((1, 6, width), lambda g: (g, 0, 0)),
            pl.BlockSpec(weight.shape, lambda g: (0, 0)),
        ],
        out_specs=(
            by_image,
            by_image,
            pl.BlockSpec((weight.shape[0], positions), lambda g: (0, g)),
            pl.BlockSpec((1, 4, width), lambda g: (g, 0, 0)),
        ),
    )


def entry_kernel(proj_ref, weight_ref, inputs_ref, middle_grad_ref, mod_ref, out_ref, sums_ref):
    grad = mm(proj_ref[...], weight_ref[...], TN)
    normed, inverse = norm_parts(inputs_ref[...].astype(FULL))
    sums_ref[0, 0:1, :] = jnp.sum(grad, axis=0, keepdims=True)
    sums_ref[0, 1:2, :] = jnp.sum(grad * normed, axis=0, keepdims=True)
    back = norm_back(grad * (1.0 + mod_ref[0, 1:2, :]), normed, inverse)
    out_ref[...] = middle_grad_ref[...] + back


def entry_backward(proj_grad, weight, inputs, middle_grad, modulation):
    images = modulation.shape[0]
    tokens, width = inputs.shape
    positions = tokens // images
    by_image = pl.BlockSpec((positions, width), lambda g: (g, 0))
    return call(
        entry_kernel,
        "entry_backward",
        (shape((tokens, width)), shape((images, 2, width))),
        (proj_grad, weight, inputs, middle_grad, modulation),
        grid=(images,),
        specs=[
            pl.BlockSpec((proj_grad.shape[0], positions), lambda g: (0, g)),
            pl.BlockSpec(weight.shape, lambda g: (0, 0)),
            by_image,
            by_image,
            pl.BlockSpec((1, 6, width), lambda g: (g, 0, 0)),
        ],
        out_specs=(by_image, pl.BlockSpec((1, 2, width), lambda g: (g, 0, 0))),
    )


def end_kernel(branch_ref, bias_ref, middle_ref, mod_ref, out_ref):
    branch = branch_ref[...] + bias_ref[...].astype(FULL)
    out_ref[...] = (middle_ref[...] + mod_ref[0, 5:6, :] * branch).astype(LOW)


def end_forward(branch, bias, middle, modulation):
    images = modulation.shape[0]
    tokens, width = middle.shape
    by_image = pl.BlockSpec((tokens // images, width), lambda g: (g, 0))
    return call(
        end_kernel,
        "end_forward",
        shape((tokens, width), LOW),
        (branch, bias, middle, modulation),
        grid=(images,),
        specs=[
            by_image,
            pl.BlockSpec((1, width), lambda g: (0, 0)),
            by_image,
            pl.BlockSpec((1, 6, width), lambda g: (g, 0, 0)),
        ],
        out_specs=by_image,
    )


def modulator_kernel(every_ref, context_ref, out_ref, sums_ref):
    part = every_ref[...]
    sums_ref[...] = jnp.sum(part, axis=0, keepdims=True)
    context = context_ref[:, : out_ref.shape[0]].astype(LOW)
    out_ref[...] = mm(context, part.astype(LOW), TN)


def modulator_backward(every, rows, context_width, width):
    images = every.shape[0]
    at = 6 * width // context_width
    return call(
        modulator_kernel,
        "modulator_backward",
        (shape((rows, 6 * width)), shape((1, 6 * width))),
        (every, every),
        grid=(6,),
        specs=[
            pl.BlockSpec((images, width), lambda p: (0, p)),
            pl.BlockSpec((images, context_width), lambda p: (0, at)),
        ],
        out_specs=(
            pl.BlockSpec((rows, width), lambda p: (0, p)),
            pl.BlockSpec((1, width), lambda p: (0, p)),
        ),
    )


def mlp_grads_kernel(place, active, branch_grad, entry, hidden_grad, away_ref, kept_ref):
    half = active.shape[1] // 2
    for ref, core in ((away_ref, 1 - place[0]), (kept_ref, place[0])):
        column = rows_at(core * half, half, 128)
        ref[:half, :] = mm(active[:, column], branch_grad[...], TN)
        ref[half:, :] = mm(entry[:, column], hidden_grad[...], TN)


def mlp_grads(place, active, branch_grad, entry, hidden_grad):
    width = entry.shape[1]
    half = shape((width, width))
    operands = (place, active, branch_grad, entry, hidden_grad)
    return call(mlp_grads_kernel, "mlp_grads", (half, half), operands, smem=1)


def attn_grads_kernel(place, proj, entry, mixed, grad, away_ref, kept_ref, sums_ref, own_ref):
    columns = mixed.shape[0]
    for j in range(3):
        own_ref[j * columns : (j + 1) * columns, :] = proj[j, rows_at(place[2] * columns, columns, 16), :]
    sums_ref[...] = mm(jnp.ones((8, own_ref.shape[1]), LOW), own_ref[...], NT)
    inner, outer = 3 * columns // 2, columns // 2
    for ref, core in ((away_ref, 1 - place[0]), (kept_ref, place[0])):
        ref[:inner, :] = mm(own_ref[rows_at(core * inner, inner, 16), :], entry[...])
        ref[inner:, :] = mm(mixed[rows_at(core * outer, outer), :].astype(LOW), grad[...])


def attn_grads(place, proj, entry, mixed, grad):
    columns, tokens = mixed.shape
    width = entry.shape[1]
    half = shape((2 * columns, width))
    return call(
        attn_grads_kernel,
        "attn_grads",
        (half, half, shape((8, 3 * columns))),
        (place, proj, entry, mixed, grad),
        smem=1,
        scratch=[pltpu.VMEM((3 * columns, tokens), LOW)],
    )


def cut_kernel(shares, place, kept, other, *outs):
    for k, out in enumerate(outs):
        base, at = 0, 0
        for share in shares:
            row = rows_at(base + (place[1] ^ k) * share, share)
            out[at : at + share, :] = kept[row, :] + other[row, :]
            base, at = base + CHIPS * share, at + share


def place_kernel(shares, place, *refs):
    parts, out = refs[:-1], refs[-1]
    for k, part in enumerate(parts):
        base, at = 0, 0
        for share in shares:
            out[rows_at(base + (place[1] ^ k) * share, share), :] = part[at : at + share, :]
            base, at = base + CHIPS * share, at + share


def whole_kernel(shares, place, mine, other, *refs):
    outs, sems = refs[:-1], refs[-1]
    base, copies = 0, []
    for share, out in zip(shares, outs):
        half = CHIPS * share
        for part, core in ((mine, place[0]), (other, 1 - place[0])):
            target = out.at[rows_at(core * half, half), :]
            source = part.at[pl.ds(base, half), :]
            copies.append(pltpu.make_async_copy(source, target, sems.at[len(copies)]))
        base += half
    for copy in copies:
        copy.start()
    for copy in copies:
        copy.wait()


def flip(value, axis, count, mask):
    return lax.ppermute(value, axis, [(i, i ^ mask) for i in range(count)])


def cut_shares(place, away, kept, shares, n_dp):
    other = flip(away, "dp", n_dp, 1)
    part = shape((sum(shares), kept.shape[1]))
    return call(
        functools.partial(cut_kernel, shares), "cut", (part,) * CHIPS, (place, kept, other), smem=1
    )


def sum_shares(parts, n_dp, *others):
    moved = [flip(parts[k], "dp", n_dp, 2 * k) for k in range(1, CHIPS)]
    total = (tie(parts[0], *others) if others else parts[0]) + moved[0] + moved[1] + moved[2]
    masks = [1 << i for i in range(3, n_dp.bit_length() - 1)]
    return double(halve(total, n_dp, masks), n_dp, masks), moved


def spread_chips(share, n_dp):
    return [share] + [flip(share, "dp", n_dp, 2 * k) for k in range(1, CHIPS)]


def own_half(place, parts, shares):
    half = shape((CHIPS * sum(shares), parts[0].shape[1]))
    return call(functools.partial(place_kernel, shares), "place", half, (place, *parts), smem=1)


def both_halves(place, mine, other, shares):
    outs = tuple(shape((GROUP * count, mine.shape[1])) for count in shares)
    anywhere = pl.BlockSpec(memory_space=pl.ANY)
    return call(
        functools.partial(whole_kernel, shares),
        "whole",
        outs,
        (place, mine, other),
        smem=1,
        specs=[pl.BlockSpec(memory_space=pltpu.VMEM)] * 2,
        out_specs=(anywhere,) * len(outs),
        scratch=[pltpu.SemaphoreType.DMA((2 * len(outs),))],
    )


def halve(value, count, masks):
    index = lax.axis_index("dp")
    for mask in masks:
        half = value.shape[0] // 2
        side = (index // mask) % 2
        away = lax.dynamic_slice_in_dim(value, (1 - side) * half, half, 0)
        kept = lax.dynamic_slice_in_dim(value, side * half, half, 0)
        value = kept + flip(away, "dp", count, mask)
    return value


def double(value, count, masks):
    index = lax.axis_index("dp")
    for mask in reversed(masks):
        other = flip(value, "dp", count, mask)
        lower = (index // mask) % 2 == 0
        value = jnp.concatenate([jnp.where(lower, value, other), jnp.where(lower, other, value)])
    return value


def core_pair(rows, n_dp):
    other = flip(rows, "dp", n_dp, 1)
    first = lax.axis_index("dp") % 2 == 0
    return jnp.concatenate([jnp.where(first, rows, other), jnp.where(first, other, rows)])


def all_pairs(pair, n_dp):
    if n_dp != GROUP:
        pairs = lax.all_gather(pair, "dp").reshape(n_dp // 2, 2, *pair.shape)
        return pairs[:, 0].reshape(-1, pair.shape[1])
    chip = lax.axis_index("dp") // 2
    parts = [pair] + [flip(pair, "dp", n_dp, 2 * k) for k in range(1, CHIPS)]
    for bit in (1, 2):
        parts = [jnp.where(chip & bit != 0, parts[k ^ bit], parts[k]) for k in range(CHIPS)]
    return jnp.concatenate(parts)


def gather_rows(rows, n_dp):
    share = rows.shape[0] // n_dp
    mine = lax.dynamic_slice_in_dim(rows, lax.axis_index("dp") * share, share, 0)
    return lax.all_gather(mine.astype(FULL), ("tensor", "dp"), tiled=True)


def gather_z(rows, n_tensor):
    share = rows.shape[0] // GROUP
    start = (lax.axis_index("dp") % GROUP) * share
    mine = lax.dynamic_slice_in_dim(rows, start, share, 0).astype(FULL)
    return [mine] + [flip(mine, "tensor", n_tensor, k) for k in range(1, n_tensor)]


def gather_pieces(parts, n_dp):
    stacked = jnp.stack(parts)
    pieces = [stacked] + [flip(stacked, "dp", n_dp, 2 * k) for k in range(1, CHIPS)]
    return pieces + [flip(piece, "dp", n_dp, 1) for piece in pieces]


def tie_kernel(*refs):
    pass


def tie(value, *others):
    anywhere = pl.BlockSpec(memory_space=pl.ANY)
    return pl.pallas_call(
        tie_kernel,
        out_shape=jax.ShapeDtypeStruct(value.shape, value.dtype),
        in_specs=[anywhere] * (1 + len(others)),
        out_specs=anywhere,
        input_output_aliases={0: 0},
        name="tie",
    )(value, *others)


def as_one(function, *operands):
    shapes = jax.eval_shape(function, *operands)
    nothing = lambda *_: jax.tree.map(lambda leaf: jnp.zeros(leaf.shape, leaf.dtype), shapes)
    return lax.cond(lax.axis_index("dp") >= 0, function, nothing, *operands)


def per_device(
    n_dp,
    n_tensor,
    latents,
    condition,
    modulator,
    modulator_bias,
    attn_input,
    attn_input_bias,
    attn_output,
    attn_output_bias,
    ffn_input,
    ffn_input_bias,
    ffn_output,
    ffn_output_bias,
    cotangent,
):
    image_count, positions, features = latents.shape
    tokens = image_count * positions
    columns = attn_input.shape[2]
    z = lax.axis_index("tensor")
    member = lax.axis_index("dp") % GROUP
    place = jnp.stack([member % 2, member // 2, z]).astype(jnp.int32)
    inputs = latents.reshape(tokens, features)
    upstream = cotangent.reshape(tokens, features)
    weight_t = attn_input.swapaxes(1, 2)

    weight_wide = gather_rows(weight_t.reshape(-1, features), n_dp)
    weight_wide = weight_wide.reshape(n_tensor, 3, columns, features)
    cond_float = condition.astype(FULL)
    context_low = jax.nn.silu(cond_float).astype(LOW)

    bias_own = jnp.stack(
        [attn_input_bias[0], jnp.zeros_like(attn_input_bias[0]), attn_input_bias[1]]
    )

    def forward(context_low):
        def start(context_low):
            shared = mm(context_low, modulator)
            shared = [shared] + [flip(shared, "tensor", n_tensor, k) for k in range(1, n_tensor)]
            results = call(
                start_kernel,
                "start",
                (
                    shape((columns, tokens)),
                    shape((tokens, features), LOW),
                    shape((image_count, 6, features)),
                ),
                (*shared, modulator_bias[None], inputs, weight_t, bias_own),
            )
            return results, shared

        output_parts = gather_z(attn_output, n_tensor)
        (mixed_t, entry_one, modulation), shared = start(context_low)
        output_parts = [tie(x, shared[-1]) for x in output_parts]
        near, far = (flip(mixed_t, "tensor", n_tensor, k) for k in (1, 2))
        inner = lax.ppermute(mixed_t, "tensor", [(1, 2), (2, 1)])
        outer = lax.ppermute(far, "tensor", [(1, 0), (2, 3)])
        mixed = [mixed_t, near, far, inner, outer]
        output_pieces = gather_pieces(output_parts, n_dp)
        attention, middle, entry_two, output_full = join_heads(
            place, mixed, output_pieces, attn_output_bias[None], inputs, modulation
        )
        hidden = mm(entry_two, ffn_input) + ffn_input_bias.astype(FULL)
        active, gelu_pull = jax.vjp(lambda inner: jax.nn.gelu(inner, approximate=True), hidden)
        active = active.astype(LOW)
        gate_two = modulation[:, None, 5]
        branch_grad = (gate_two * cotangent.astype(FULL)).astype(LOW).reshape(tokens, features)
        hidden_grad = gelu_pull(mm(branch_grad, ffn_output, NT))[0].astype(LOW)
        first = mixed_t, entry_one, modulation, attention, middle, output_full
        return first, (active, branch_grad, entry_two, hidden_grad)

    first, mlp = as_one(forward, context_low)
    part = mm(mlp[3], ffn_input, NT)
    mixed_t, entry_one, modulation, attention, middle, output_full = first
    entry_two_grad = lax.psum(part, "tensor")
    mlp_shares = (ffn_output.shape[0] // GROUP, features // GROUP)

    def beside_entry_two(place, mlp):
        active, branch_grad, entry_two, hidden_grad = mlp
        away, kept = mlp_grads(place, active, branch_grad, entry_two, hidden_grad)
        mlp_share = sum_shares(cut_shares(place, away, kept, mlp_shares, n_dp), n_dp)[0]
        branch_part = mm(active, ffn_output)
        weights = cotangent.astype(FULL)
        gate_part = jnp.sum(weights * branch_part.reshape(latents.shape), axis=1)
        bias_row = jnp.zeros((3, n_tensor * columns), FULL)
        bias_row = lax.dynamic_update_slice_in_dim(bias_row, bias_own.astype(FULL), z * columns, 1)
        part = jnp.concatenate([gate_part, bias_row])
        parts = [part] + [flip(part, "tensor", n_tensor, k) for k in range(1, n_tensor)]
        part = (parts[0] + parts[1]) + (parts[2] + parts[3])
        gate_grad = part[:image_count] + ffn_output_bias.astype(FULL) * jnp.sum(weights, axis=1)
        sums = [jnp.sum(x.astype(FULL), axis=0) for x in (branch_grad, hidden_grad)]
        return mlp_share, branch_part, gate_grad, part[image_count:], sums

    mlp_share, branch_part, gate_two_grad, bias_full, mlp_sums = as_one(
        beside_entry_two, tie(place, part), mlp
    )

    def still_beside_entry_two(weight_wide, mlp_share):
        mlp_parts = spread_chips(mlp_share, n_dp)
        proj_full, weight_full = project_all(weight_wide, bias_full, entry_one)
        return mlp_parts, all_probs(proj_full, image_count), proj_full, weight_full

    mlp_parts, probs, proj_full, weight_full = as_one(
        still_beside_entry_two, tie(weight_wide, branch_part), mlp_share
    )
    entry_two_grad = tie(entry_two_grad, probs)
    entry_two_grad = tie(entry_two_grad, branch_part)
    branch_part = tie(branch_part, entry_two_grad)
    branch = lax.psum(branch_part, "tensor")
    attn_shares = (3 * columns // GROUP, columns // GROUP)

    def beside_branch(
        entry_two_grad, probs, proj_full, weight_full, gate_two_grad, mlp_sums, mlp_parts
    ):
        def heads(entry_two_grad, probs, proj_full):
            middle_grad, attention_grad, mixed_grad_t, middle_sums = middle_backward(
                entry_two_grad, middle, attention, upstream, modulation, output_full
            )
            proj_grad = attention_backward(probs, proj_full, mixed_grad_t)
            parts = attn_grads(place, proj_grad, entry_one, mixed_t, attention_grad)
            return middle_grad, middle_sums, proj_grad, parts

        middle_grad, middle_sums, proj_grad, (away, kept, own_sums) = as_one(
            heads, entry_two_grad, probs, proj_full
        )
        parts = cut_shares(place, away, kept, attn_shares, n_dp)

        def entry(proj_grad, weight_full, middle_grad):
            return entry_backward(
                proj_grad.reshape(-1, tokens),
                weight_full.reshape(-1, features),
                inputs,
                middle_grad,
                modulation,
            )

        latents_grad, entry_sums = as_one(
            entry, tie(proj_grad, parts[0]), weight_full, middle_grad
        )
        mlp_mine = own_half(place, [tie(mlp_parts[0], away), *mlp_parts[1:]], mlp_shares)
        mlp_other = flip(mlp_mine, "dp", n_dp, 1)
        modulation_grad = jnp.concatenate(
            [entry_sums, middle_sums[:, :3], gate_two_grad[:, None]], axis=1
        )
        modulation_grad = modulation_grad.reshape(image_count, -1).astype(LOW)
        attn_share, moved = sum_shares(parts, n_dp, entry_sums)
        sums = [mlp_sums[0], mlp_sums[1], jnp.sum(middle_sums[:, 3], axis=0), own_sums[0]]
        sizes = [x.shape[0] for x in sums]
        sums = jnp.pad(jnp.concatenate(sums)[None], ((0, image_count - 1), (0, 0)))
        context_wide = jnp.pad(context_low.astype(FULL), ((0, 0), (0, -context_low.shape[1] % 256)))
        small = [modulation_grad.astype(FULL), context_wide, sums]
        pair = core_pair(tie(jnp.concatenate(small, axis=1), *moved), n_dp)
        every = all_pairs(pair, n_dp)
        attn_parts = spread_chips(tie(attn_share, pair), n_dp)

        def finish(every, modulation_grad, mlp_mine, mlp_other):
            grad_modulator, grad_modulator_bias = modulator_backward(
                every, context_low.shape[1], context_wide.shape[1], features
            )
            sums = jnp.sum(every[:, 6 * features + context_wide.shape[1] :], axis=0)
            sums = jnp.split(sums, [sum(sizes[:i]) for i in (1, 2, 3)])
            context_grad = mm(modulation_grad, modulator, NT)
            condition_grad = jax.vjp(jax.nn.silu, cond_float)[1](context_grad)[0]
            mlp_whole = both_halves(place, mlp_mine, mlp_other, mlp_shares)
            return (grad_modulator, grad_modulator_bias), sums, condition_grad, mlp_whole

        modulator_grads, sums, condition_grad, mlp_whole = as_one(
            finish, every, modulation_grad, mlp_mine, mlp_other
        )
        attn_parts[0] = tie(attn_parts[0], condition_grad)
        attn_mine = own_half(place, attn_parts, attn_shares)
        attn_whole = both_halves(place, attn_mine, flip(attn_mine, "dp", n_dp, 1), attn_shares)
        return mlp_whole, attn_whole, latents_grad, condition_grad, modulator_grads, sums

    mlp_whole, attn_whole, latents_grad, condition_grad, modulator_grads, sums = as_one(
        beside_branch,
        tie(entry_two_grad, branch_part),
        probs,
        proj_full,
        weight_full,
        gate_two_grad,
        mlp_sums,
        mlp_parts,
    )
    grad_modulator, grad_modulator_bias = modulator_grads
    layer_out = end_forward(
        tie(branch, condition_grad), ffn_output_bias[None], middle, modulation
    )
    input_bias = sums[3].reshape(3, columns)
    return (
        layer_out.reshape(latents.shape),
        latents_grad.reshape(latents.shape),
        condition_grad,
        grad_modulator,
        grad_modulator_bias[0],
        attn_whole[0].reshape(3, columns, features).swapaxes(1, 2),
        jnp.stack([input_bias[0], input_bias[2]]),
        attn_whole[1],
        sums[2],
        mlp_whole[1],
        sums[1],
        mlp_whole[0],
        sums[0],
    )


def solution(mesh):
    placed = (
        P("dp", None, None),
        P("dp", "tensor"),
        P("tensor", None),
        P(),
        P(None, None, "tensor"),
        P(None, "tensor"),
        P("tensor", None),
        P(),
        P(None, "tensor"),
        P("tensor"),
        P("tensor", None),
        P(),
        P("dp", None, None),
    )
    return jax.shard_map(
        functools.partial(per_device, mesh.shape["dp"], mesh.shape["tensor"]),
        mesh=mesh,
        in_specs=placed,
        out_specs=(
            P("dp", None, None),
            P("dp", None, None),
            P("dp", "tensor"),
            P("tensor", None),
            P(),
            P(None, None, "tensor"),
            P(None, "tensor"),
            P("tensor", None),
            P(),
            P(None, "tensor"),
            P("tensor"),
            P("tensor", None),
            P(),
        ),
        check_vma=False,
    )
```
